32 devices in a mesh: vec: 4 (over y, core), row: 2 (over x), col: 4 (over z).
Axes of the slice: x: 2, y: 2, z: 4, core: 2. Of those that a mesh axis runs over, the one named last changes fastest.
Arguments:
- checkpoints: float32 [2, 2, 16, 64, 512], P(None, None, 'vec', 'row', 'col'), may hold values from -6 to 6
- adjoints_in: float32 [2, 16, 64, 512], P(None, 'vec', 'row', 'col'), may hold values from -4 to 4
- vector_bits: int32 [16, 64, 512], P('vec', 'row', 'col'), may hold values 0 or 1
- potential_int: int32 [64, 512], P('row', 'col'), may hold values from -32767 to 32767
- pot_scale: float32 [1], replicated, may hold values from 1.5e-05 to 9e-05
- energies: float32 [16], replicated, may hold values from -0.9 to 0.9
- residual: float32 [16, 64, 512], P(None, 'row', 'col'), may hold values from -6 to 6
- first_segment: int32 [1], replicated, may hold values from 0 to 62
Outputs:
- potential_grad: float32 [64, 512], P('row', 'col')
- adjoint_out: float32 [2, 16, 64, 512], P(None, 'vec', 'row', 'col')
The draws below stay inside these ranges and needn't reach their ends.
All inputs are finite; a program needn't handle non-finite values. No bound on the sum of `vector_bits` on one device may be relied on, other than what follows from the above.
Results may differ from the reference program's by a relative error of at most 0.0003.
Values sent between devices are 32-bit elements; how exact they have to be, the bound alone decides.
A program may use at most 64 MiB of HBM per device.

```python
import math
import jax
import jax.numpy as jnp
from jax import lax

VEC_DEV = 4
SEG = 16
MOMENTS = 1024
ENERGIES = 16
QMAX = 32767
NR = 64
NC = 512
NVEC = 16


def plant(result, stream_key, least, largest):
    index_at = [jax.random.randint(jax.random.fold_in(stream_key, axis), (), 0, length) for axis, length in enumerate(result.shape)]
    longest = result.shape.index(max(result.shape))
    next_to = index_at[:longest] + [(index_at[longest] + 1) % result.shape[longest]] + index_at[longest + 1:]
    return result.at[tuple(index_at)].set(least).at[tuple(next_to)].set(largest)


def levels(stream_key, extent, pieces, low, high):
    gain, own = 1.0, jax.random.fold_in(stream_key, 6)
    for axis_at, parts in pieces:
        draws = jnp.exp(jax.random.uniform(jax.random.fold_in(own, axis_at), (parts,), jnp.float32, low / len(pieces), high / len(pieces)))
        gain = gain * jnp.repeat(draws, extent[axis_at] // parts).reshape([-1 if axis == axis_at else 1 for axis in range(len(extent))])
    return gain


def scatter_about(stream_key, shape, width, limit, shards=(), kind=jnp.bfloat16):
    gain = levels(stream_key, shape, shards, -0.22, 0.18) if shards else 1.0
    array = jax.random.normal(stream_key, shape, jnp.float32) * width * gain
    return jnp.minimum(jnp.maximum(array, -limit), limit).astype(kind)


def setup_inputs(seed: int = 0) -> dict:
    key_list = jax.random.split(jax.random.key(seed), 9)
    return {
        "checkpoints": scatter_about(key_list[0], (2, 2, NVEC, NR, NC), 1.0, 6.0, ((2, 4), (3, 2), (4, 4)), jnp.float32),
        "adjoints_in": scatter_about(key_list[1], (2, NVEC, NR, NC), 0.3, 4.0, ((1, 4), (2, 2), (3, 4)), jnp.float32),
        "vector_bits": plant((jax.random.randint(key_list[2], (NVEC, NR, NC), 0, 2) < 1).astype(jnp.int32), jax.random.fold_in(key_list[2], 1), 0, 1),
        "potential_int": plant(jax.random.randint(key_list[3], (NR, NC), -QMAX, QMAX + 1), jax.random.fold_in(key_list[3], 1), -QMAX, QMAX).astype(jnp.int32),
        "pot_scale": jnp.clip(jnp.exp(jax.random.uniform(key_list[4], (1,), jnp.float32, math.log(1.4999999621068127e-05), math.log(9.000000136438757e-05))), 1.4999999621068127e-05, 9.000000136438757e-05),
        "energies": jnp.clip(jax.random.uniform(key_list[5], (ENERGIES,), jnp.float32, -0.9, 0.9), -0.9, 0.9),
        "residual": scatter_about(key_list[6], (ENERGIES, NR, NC), 1.0, 6.0, ((1, 2), (2, 4)), jnp.float32),
        "first_segment": jax.random.randint(key_list[7], (1,), 0, MOMENTS // SEG - 1).astype(jnp.int32),
    }


def window_coefs(first_segment, energies):
    moment_order = first_segment[0] * SEG + jnp.arange(2 * SEG, dtype=jnp.int32)
    degree = moment_order.astype(jnp.float32)
    kernel_norm = float(MOMENTS + 1)
    angle_step = math.pi / kernel_norm
    jackson = ((kernel_norm - degree) * jnp.cos(angle_step * degree) + jnp.sin(angle_step * degree) * (math.cos(angle_step) / math.sin(angle_step))) / kernel_norm
    factor = jnp.where(moment_order == 0, 1.0, 2.0).astype(jnp.float32)
    angles = jnp.arccos(energies)
    cosines = jnp.cos(degree[:, None] * angles[None, :])
    return (jackson * factor)[:, None] * cosines / (math.pi * jnp.sin(angles))[None, :]


def apply_operator(values, onsite, inv_span):
    beside = jnp.roll(values, 1, -2) + jnp.roll(values, -1, -2) + jnp.roll(values, 1, -1) + jnp.roll(values, -1, -1)
    return inv_span * (onsite * values - beside)


def reference(checkpoints, adjoints_in, vector_bits, potential_int, pot_scale, energies, residual, first_segment):
    pot_factor = pot_scale[0]
    inv_span = 1.0 / (4.5 + QMAX * pot_factor)
    onsite = potential_int.astype(jnp.float32) * pot_factor
    coefficients = window_coefs(first_segment, energies)
    weights = jnp.einsum("ne,eij->nij", coefficients, residual, precision=lax.Precision.HIGHEST)
    inv_count = 1.0 / NVEC
    gradient = jnp.zeros((NR, NC), jnp.float32)
    adjoint_blocks = []
    for first_vec in range(0, NVEC, VEC_DEV):
        saved = checkpoints[:, :, first_vec:first_vec + VEC_DEV]
        sign_weights = (2 * vector_bits[first_vec:first_vec + VEC_DEV] - 1).astype(jnp.float32) * inv_count
        states = []
        for segment in range(2):
            earlier = saved[segment, 0]
            current = saved[segment, 1]
            states.extend([earlier, current])
            for offset in range(2, SEG):
                advanced = 2.0 * apply_operator(current, onsite, inv_span) - earlier
                states.append(advanced)
                earlier, current = current, advanced
        after_one = adjoints_in[0, first_vec:first_vec + VEC_DEV]
        after_two = adjoints_in[1, first_vec:first_vec + VEC_DEV]
        for offset in range(2 * SEG - 1, -1, -1):
            gradient = gradient + jnp.sum(after_one * states[offset], axis=0)
            advanced = weights[offset] * sign_weights + 2.0 * apply_operator(after_one, onsite, inv_span) - after_two
            after_two, after_one = after_one, advanced
        adjoint_blocks.append(jnp.stack([after_one, after_two]))
    return gradient * (2.0 * inv_span), jnp.concatenate(adjoint_blocks, axis=1)
```

```python
import math

import jax
import jax.numpy as jnp
from jax import lax
from jax.experimental import pallas as pl
from jax.experimental.pallas import tpu as pltpu
from jax.sharding import PartitionSpec as P

SEG = 16
MOMENTS = 1024
QMAX = 32767


def extended_2(value, sides, width):
    for axis, dim in sides:
        devices, length = (lax.axis_size(axis), value.shape[dim])
        up = [(i, (i + 1) % devices) for i in range(devices)]
        down = [(j, i) for i, j in up]
        last = lax.slice_in_dim(value, length - width, length, axis=dim)
        initial = lax.slice_in_dim(value, 0, width, axis=dim)
        before = lax.ppermute(last, axis, up)
        after = lax.ppermute(initial, axis, down)
        value = jnp.concatenate([before, value, after], axis=dim)
    return value


def window_coefs(first_segment, energies):
    moment_order = first_segment[0] * SEG + jnp.arange(2 * SEG, dtype=jnp.int32)
    degree = moment_order.astype(jnp.float32)
    kernel_norm = float(MOMENTS + 1)
    angle_step = math.pi / kernel_norm
    jackson = (
        (kernel_norm - degree) * jnp.cos(angle_step * degree)
        + jnp.sin(angle_step * degree) * (math.cos(angle_step) / math.sin(angle_step))
    ) / kernel_norm
    factor = jnp.where(moment_order == 0, 1.0, 2.0).astype(jnp.float32)
    angles = jnp.arccos(energies)
    cosines = jnp.cos(degree[:, None] * angles[None, :])
    return (jackson * factor)[:, None] * cosines / (math.pi * jnp.sin(angles))[None, :]


def stencil(extended, onsite, inv_span):
    middle = extended[..., 1:-1, 1:-1]
    beside = (
        extended[..., 2:, 1:-1]
        + extended[..., :-2, 1:-1]
        + extended[..., 1:-1, 2:]
        + extended[..., 1:-1, :-2]
    )
    return inv_span * (onsite * middle - beside)


def per_device(
    checkpoints,
    adjoints_in,
    vector_bits,
    potential_int,
    pot_scale,
    energies,
    residual,
    first_segment,
):
    pot_factor = pot_scale[0]
    inv_span = 1.0 / (4.5 + QMAX * pot_factor)
    onsite = potential_int.astype(jnp.float32) * pot_factor
    coefficients = window_coefs(first_segment, energies)
    vector_count = lax.axis_size("vec") * vector_bits.shape[0]
    inv_count = 1.0 / vector_count
    sign_weights = (2 * vector_bits - 1).astype(jnp.float32) * inv_count
    earlier = checkpoints[:, 0]
    current = checkpoints[:, 1]
    zero_grad = jnp.zeros(onsite.shape, jnp.float32)
    carried = (adjoints_in[0], adjoints_in[1], zero_grad)
    weights = jnp.einsum("ne,eij->nij", coefficients, residual, precision=lax.Precision.HIGHEST)

    def forward_step(pair_state, unused):
        before, now = pair_state
        padded = extended_2(now, (("row", 2), ("col", 3)), 1)
        advanced = 2.0 * stencil(padded, onsite, inv_span) - before
        return ((now, advanced), advanced)

    _, generated = lax.scan(forward_step, (earlier, current), None, length=SEG - 2)
    states = jnp.concatenate([earlier[None], current[None], generated], axis=0)

    def adjoint_step(step_carry, inputs):
        after_one, after_two, accum_grad = step_carry
        state_now, weight_now = inputs
        padded = extended_2(after_one, (("row", 1), ("col", 2)), 1)
        accum_grad = accum_grad + jnp.sum(after_one * state_now, axis=0)
        advanced = weight_now * sign_weights + 2.0 * stencil(padded, onsite, inv_span) - after_two
        return ((advanced, after_one, accum_grad), None)

    for segment in (1, 0):
        carried, _ = lax.scan(
            adjoint_step,
            carried,
            (states[:, segment], weights[segment * SEG : (segment + 1) * SEG]),
            reverse=True,
        )
    adjoint_zero, adjoint_first, accum_grad = carried
    gradient = lax.psum(accum_grad, "vec") * (2.0 * inv_span)
    return (gradient, jnp.stack([adjoint_zero, adjoint_first]))


MESH = pl.DeviceIdType.MESH
TERMS = 2 * SEG
ROWS = 32
LANES = 128
REACH = 32
DEPTH = 8
ENERGIES = 16
X_CK, X_ADJ, X_BITS, X_POT, X_RES, X_GRAD, X_OUT = range(7)
Z_CK, Z_ADJ, Z_RES = range(3)
Z_PARTS = ((0, 2), (2, 2), (4, 4))
PACKS = 8


def pick_quarter(lane, parts):
    low = jnp.where(lane < REACH, parts[0], parts[1])
    high = jnp.where(lane < 3 * REACH, parts[2], parts[3])
    return jnp.where(lane < 2 * REACH, low, high)


def turn(value, shift):
    shift = shift % LANES
    return value if shift == 0 else pltpu.roll(value, shift, 1)


def kernel(
    scal, kron, ck, adj, bits, pot, res, grad_out, adj_out,
    wck, wadj, wbits, wpot, wres, zsend, zrecv, states, adjs, onsite, signs, rwin, weights,
    gbuf, gother, gall, obuf, xs, xr, zs, zr, vs, vr,
):
    x = lax.axis_index("row")
    z = lax.axis_index("col")
    y = lax.axis_index("vec")
    n_z = lax.axis_size("col")
    n_y = lax.axis_size("vec")
    across = {"row": 1 - x}
    right = {"col": lax.rem(z + 1, n_z)}
    left = {"col": lax.rem(z + n_z - 1, n_z)}
    peers = [{"vec": lax.rem(y + d, n_y)} for d in range(1, n_y)]

    barrier = pltpu.get_barrier_semaphore()
    for device in [across, right, left] + peers:
        pl.semaphore_signal(barrier, inc=1, device_id=device, device_id_type=MESH)
    pl.semaphore_wait(barrier, 3 + len(peers))

    def remote(source, target, send, recv, device):
        copy = pltpu.make_async_remote_copy(
            src_ref=source, dst_ref=target, send_sem=send, recv_sem=recv,
            device_id=device, device_id_type=MESH,
        )
        copy.start()
        return copy

    def to_x(source, target, index):
        return remote(source, target, xs.at[index], xr.at[index], across)

    theirs = pl.ds(2 * (1 - x), 2)
    mine = pl.ds(2 * x, 2)
    other = pl.ds(ROWS, ROWS)
    own = pl.ds(0, ROWS)
    c_ck = to_x(ck.at[:, :, theirs], wck.at[:, :, :, other], X_CK)
    c_adj = to_x(adj.at[:, theirs], wadj.at[:, :, other], X_ADJ)
    c_bits = to_x(bits.at[theirs], wbits.at[:, other], X_BITS)
    c_pot = to_x(pot, wpot.at[other], X_POT)
    c_res = to_x(res, wres.at[:, other], X_RES)

    wck[:, :, :, own] = ck[:, :, mine]
    wadj[:, :, own] = adj[:, mine]
    wbits[:, own] = bits[mine]
    wpot[own] = pot[...]
    wres[:, own] = res[...]

    lane = lax.broadcasted_iota(jnp.int32, (8, LANES), 1)

    def rows(j):
        return pl.ds(j, 8, stride=8)

    def pack(slot, j, planes):
        zsend[0, slot, j] = pick_quarter(lane, [turn(p, REACH * (q + 1)) for q, p in enumerate(planes)])
        zsend[1, slot, j] = pick_quarter(lane, [turn(p, REACH * q) for q, p in enumerate(planes)])

    def unpack(slot, j, q):
        from_left = turn(zrecv[0, slot, j], LANES - REACH - REACH * q)
        from_right = turn(zrecv[1, slot, j], LANES - REACH * q)
        return jnp.where(lane < 2 * REACH, from_right, from_left)

    def to_z(part):
        first, count = Z_PARTS[part]
        span = pl.ds(first, count)
        return [
            remote(zsend.at[d, span], zrecv.at[d, span], zs.at[d, part], zr.at[d, part], device)
            for d, device in enumerate((right, left))
        ]

    c_ck.wait()
    for j in range(DEPTH):
        for s in range(2):
            planes = [wck[s, k, v, rows(j)] for k in range(2) for v in range(2)]
            pack(s, j, planes)
            for q, plane in enumerate(planes):
                states[s * SEG + q // 2, q % 2, j, 0] = plane
    z_ck = to_z(Z_CK)

    pot_factor = scal[0]
    twice = scal[1]
    inv_count = scal[2]
    c_adj.wait()
    c_bits.wait()
    c_pot.wait()
    for j in range(DEPTH):
        planes = [wadj[k, v, rows(j)] for k in range(2) for v in range(2)]
        pack(2, j, planes)
        for q, plane in enumerate(planes):
            adjs[TERMS + q // 2, q % 2, j, 0] = plane
        sign = [(2 * wbits[v, rows(j)] - 1).astype(jnp.float32) * inv_count for v in range(2)]
        site = wpot[rows(j)].astype(jnp.float32) * pot_factor * twice
        pack(3, j, [sign[0], sign[1], site, site])
        signs[0, j, 0] = sign[0]
        signs[1, j, 0] = sign[1]
        onsite[j, 0] = site
    z_adj = to_z(Z_ADJ)

    c_res.wait()
    for j in range(DEPTH):
        for p in range(4):
            planes = [wres[4 * p + q, rows(j)] for q in range(4)]
            pack(4 + p, j, planes)
            for q, plane in enumerate(planes):
                rwin[j, 0, 4 * p + q] = plane
    z_res = to_z(Z_RES)

    def settle(copies):
        for copy in copies:
            copy.wait()

    settle(z_ck)
    for j in range(DEPTH):
        for s in range(2):
            for q in range(4):
                states[s * SEG + q // 2, q % 2, j, 1] = unpack(s, j, q)
    settle(z_adj)
    for j in range(DEPTH):
        for q in range(4):
            adjs[TERMS + q // 2, q % 2, j, 1] = unpack(2, j, q)
        signs[0, j, 1] = unpack(3, j, 0)
        signs[1, j, 1] = unpack(3, j, 1)
        onsite[j, 1] = unpack(3, j, 2)

    first_lane = lane == 0
    last_lane = lane == LANES - 1

    def beside(ref, t, v, j):
        here = [ref[t, v, j, c] for c in range(2)]
        back = [pltpu.roll(w, 1, 1) for w in here]
        ahead = [pltpu.roll(w, LANES - 1, 1) for w in here]
        sums = []
        for c in range(2):
            before = jnp.where(first_lane, back[1 - c], back[c])
            after = jnp.where(last_lane, ahead[1 - c], ahead[c])
            if j == 0:
                above = pltpu.roll(ref[t, v, DEPTH - 1, c], 1, 0)
            else:
                above = ref[t, v, j - 1, c]
            if j == DEPTH - 1:
                below = pltpu.roll(ref[t, v, 0, c], 7, 0)
            else:
                below = ref[t, v, j + 1, c]
            sums.append((above + below) + (before + after))
        return here, sums

    def forward(k, carry):
        for s in range(2):
            t = s * SEG + k
            for v in range(2):
                for j in range(DEPTH):
                    here, sums = beside(states, t - 1, v, j)
                    for c in range(2):
                        states[t, v, j, c] = (onsite[j, c] * here[c] - twice * sums[c]) - states[t - 2, v, j, c]
        return carry

    lax.fori_loop(2, SEG, forward, 0)

    def halves(value):
        high = value.astype(jnp.bfloat16)
        return high, (value - high.astype(jnp.float32)).astype(jnp.bfloat16)

    kron_high, kron_low = halves(kron[...])

    def weigh(c):
        for j in range(DEPTH):
            high, low = halves(rwin[j, c].reshape(ENERGIES * 8, LANES))
            dot = lambda a, b: jnp.dot(a, b, preferred_element_type=jnp.float32)
            total = dot(kron_high, high) + (dot(kron_high, low) + dot(kron_low, high))
            weights[j, c] = total.reshape(TERMS, 8, LANES)

    weigh(0)
    settle(z_res)
    for j in range(DEPTH):
        for p in range(4):
            for q in range(4):
                rwin[j, 1, 4 * p + q] = unpack(4 + p, j, q)
    weigh(1)

    def adjoint(i, sums_in):
        t = TERMS - 1 - i
        grads = list(sums_in)
        for v in range(2):
            for j in range(DEPTH):
                here, sums = beside(adjs, t + 1, v, j)
                grads[j] = grads[j] + here[0] * states[t, v, j, 0]
                for c in range(2):
                    source = weights[j, c, t] * signs[v, j, c]
                    adjs[t, v, j, c] = (source + onsite[j, c] * here[c]) - (twice * sums[c] + adjs[t + 2, v, j, c])
        return tuple(grads)

    zero = jnp.zeros((8, LANES), jnp.float32)
    grads = lax.fori_loop(0, TERMS, adjoint, (zero,) * DEPTH)

    for j in range(DEPTH):
        gbuf[rows(j)] = grads[j]
        for k in range(2):
            for v in range(2):
                obuf[k, v, rows(j)] = adjs[k, v, j, 0]
    c_grad = to_x(gbuf.at[other], gother, X_GRAD)
    c_out = to_x(obuf.at[:, :, other], adj_out.at[:, mine], X_OUT)
    adj_out[:, mine] = obuf[:, :, own]
    c_grad.wait()
    gall[y] = gbuf[own] + gother[...]
    shares = [
        remote(gall.at[y], gall.at[y], vs.at[d], vr.at[d], device) for d, device in enumerate(peers)
    ]
    settle(shares)
    total = gall[0]
    for d in range(1, n_y):
        total = total + gall[d]
    grad_out[...] = total * twice
    c_out.wait()


def windowed(
    checkpoints,
    adjoints_in,
    vector_bits,
    potential_int,
    pot_scale,
    energies,
    residual,
    first_segment,
):
    n_y = lax.axis_size("vec")
    pot_factor = pot_scale[0]
    twice = 2.0 / (4.5 + QMAX * pot_factor)
    coefficients = window_coefs(first_segment, energies)
    inv_count = 1.0 / (n_y * vector_bits.shape[0])
    scal = jnp.stack([pot_factor, twice, jnp.float32(inv_count)])
    spread = coefficients[:, None, :, None] * jnp.eye(8, dtype=jnp.float32)[None, :, None, :]
    spread = spread.reshape(TERMS * 8, ENERGIES * 8)
    kron = spread
    f32, i32 = jnp.float32, jnp.int32
    vmem = pl.BlockSpec(memory_space=pltpu.VMEM)
    tile = (8, LANES)
    gradient, adjoint_out = pl.pallas_call(
        kernel,
        out_shape=(
            jax.ShapeDtypeStruct(potential_int.shape, f32),
            jax.ShapeDtypeStruct(adjoints_in.shape, f32),
        ),
        in_specs=[pl.BlockSpec(memory_space=pltpu.SMEM)] + [vmem] * 6,
        out_specs=(vmem, vmem),
        scratch_shapes=[
            pltpu.VMEM((2, 2, 2, 2 * ROWS, LANES), f32),
            pltpu.VMEM((2, 2, 2 * ROWS, LANES), f32),
            pltpu.VMEM((2, 2 * ROWS, LANES), i32),
            pltpu.VMEM((2 * ROWS, LANES), i32),
            pltpu.VMEM((ENERGIES, 2 * ROWS, LANES), f32),
            pltpu.VMEM((2, PACKS, DEPTH) + tile, f32),
            pltpu.VMEM((2, PACKS, DEPTH) + tile, f32),
            pltpu.VMEM((TERMS, 2, DEPTH, 2) + tile, f32),
            pltpu.VMEM((TERMS + 2, 2, DEPTH, 2) + tile, f32),
            pltpu.VMEM((DEPTH, 2) + tile, f32),
            pltpu.VMEM((2, DEPTH, 2) + tile, f32),
            pltpu.VMEM((DEPTH, 2, ENERGIES) + tile, f32),
            pltpu.VMEM((DEPTH, 2, TERMS) + tile, f32),
            pltpu.VMEM((2 * ROWS, LANES), f32),
            pltpu.VMEM((ROWS, LANES), f32),
            pltpu.VMEM((n_y, ROWS, LANES), f32),
            pltpu.VMEM((2, 2, 2 * ROWS, LANES), f32),
            pltpu.SemaphoreType.DMA((7,)),
            pltpu.SemaphoreType.DMA((7,)),
            pltpu.SemaphoreType.DMA((2, 3)),
            pltpu.SemaphoreType.DMA((2, 3)),
            pltpu.SemaphoreType.DMA((n_y - 1,)),
            pltpu.SemaphoreType.DMA((n_y - 1,)),
        ],
        compiler_params=pltpu.CompilerParams(
            collective_id=0, has_side_effects=True, vmem_limit_bytes=40 * 1024 * 1024
        ),
    )(scal, kron, checkpoints, adjoints_in, vector_bits, potential_int, residual)
    return gradient, adjoint_out


def solution(mesh):
    fits = mesh.shape["row"] == 2 and mesh.shape["col"] > 2
    return jax.shard_map(
        windowed if fits else per_device,
        mesh=mesh,
        in_specs=(
            P(None, None, "vec", "row", "col"),
            P(None, "vec", "row", "col"),
            P("vec", "row", "col"),
            P("row", "col"),
            P(),
            P(),
            P(None, "row", "col"),
            P(),
        ),
        out_specs=(P("row", "col"), P(None, "vec", "row", "col")),
        check_vma=False,
    )
```

```python
import math

import jax
import jax.numpy as jnp
from jax import lax
from jax.experimental import pallas as pl
from jax.experimental.pallas import tpu as pltpu
from jax.sharding import PartitionSpec as P

SEG = 16
MOMENTS = 1024
QMAX = 32767


def extended_2(value, sides, width):
    for axis, dim in sides:
        devices, length = (lax.axis_size(axis), value.shape[dim])
        up = [(i, (i + 1) % devices) for i in range(devices)]
        down = [(j, i) for i, j in up]
        last = lax.slice_in_dim(value, length - width, length, axis=dim)
        initial = lax.slice_in_dim(value, 0, width, axis=dim)
        before = lax.ppermute(last, axis, up)
        after = lax.ppermute(initial, axis, down)
        value = jnp.concatenate([before, value, after], axis=dim)
    return value


def window_coefs(first_segment, energies):
    moment_order = first_segment[0] * SEG + jnp.arange(2 * SEG, dtype=jnp.int32)
    degree = moment_order.astype(jnp.float32)
    kernel_norm = float(MOMENTS + 1)
    angle_step = math.pi / kernel_norm
    jackson = (
        (kernel_norm - degree) * jnp.cos(angle_step * degree)
        + jnp.sin(angle_step * degree) * (math.cos(angle_step) / math.sin(angle_step))
    ) / kernel_norm
    factor = jnp.where(moment_order == 0, 1.0, 2.0).astype(jnp.float32)
    angles = jnp.arccos(energies)
    cosines = jnp.cos(degree[:, None] * angles[None, :])
    return (jackson * factor)[:, None] * cosines / (math.pi * jnp.sin(angles))[None, :]


def stencil(extended, onsite, inv_span):
    middle = extended[..., 1:-1, 1:-1]
    beside = (
        extended[..., 2:, 1:-1]
        + extended[..., :-2, 1:-1]
        + extended[..., 1:-1, 2:]
        + extended[..., 1:-1, :-2]
    )
    return inv_span * (onsite * middle - beside)


def per_device(
    checkpoints,
    adjoints_in,
    vector_bits,
    potential_int,
    pot_scale,
    energies,
    residual,
    first_segment,
):
    pot_factor = pot_scale[0]
    inv_span = 1.0 / (4.5 + QMAX * pot_factor)
    onsite = potential_int.astype(jnp.float32) * pot_factor
    coefficients = window_coefs(first_segment, energies)
    vector_count = lax.axis_size("vec") * vector_bits.shape[0]
    inv_count = 1.0 / vector_count
    sign_weights = (2 * vector_bits - 1).astype(jnp.float32) * inv_count
    earlier = checkpoints[:, 0]
    current = checkpoints[:, 1]
    zero_grad = jnp.zeros(onsite.shape, jnp.float32)
    carried = (adjoints_in[0], adjoints_in[1], zero_grad)
    weights = jnp.einsum("ne,eij->nij", coefficients, residual, precision=lax.Precision.HIGHEST)

    def forward_step(pair_state, unused):
        before, now = pair_state
        padded = extended_2(now, (("row", 2), ("col", 3)), 1)
        advanced = 2.0 * stencil(padded, onsite, inv_span) - before
        return ((now, advanced), advanced)

    _, generated = lax.scan(forward_step, (earlier, current), None, length=SEG - 2)
    states = jnp.concatenate([earlier[None], current[None], generated], axis=0)

    def adjoint_step(step_carry, inputs):
        after_one, after_two, accum_grad = step_carry
        state_now, weight_now = inputs
        padded = extended_2(after_one, (("row", 1), ("col", 2)), 1)
        accum_grad = accum_grad + jnp.sum(after_one * state_now, axis=0)
        advanced = weight_now * sign_weights + 2.0 * stencil(padded, onsite, inv_span) - after_two
        return ((advanced, after_one, accum_grad), None)

    for segment in (1, 0):
        carried, _ = lax.scan(
            adjoint_step,
            carried,
            (states[:, segment], weights[segment * SEG : (segment + 1) * SEG]),
            reverse=True,
        )
    adjoint_zero, adjoint_first, accum_grad = carried
    gradient = lax.psum(accum_grad, "vec") * (2.0 * inv_span)
    return (gradient, jnp.stack([adjoint_zero, adjoint_first]))


MESH = pl.DeviceIdType.MESH
TERMS = 2 * SEG
ROWS = 32
LANES = 128
REACH = 32
DEPTH = 8
ENERGIES = 16
X_CK, X_ADJ, X_BITS, X_POT, X_RES, X_GRAD, X_OUT = range(7)
Z_CK, Z_ADJ, Z_RES = range(3)
Z_PARTS = ((0, 2), (2, 2), (4, 4))
PACKS = 8


def pick_quarter(lane, parts):
    low = jnp.where(lane < REACH, parts[0], parts[1])
    high = jnp.where(lane < 3 * REACH, parts[2], parts[3])
    return jnp.where(lane < 2 * REACH, low, high)


def turn(value, shift):
    shift = shift % LANES
    return value if shift == 0 else pltpu.roll(value, shift, 1)


def kernel(
    scal, coefs, ck, adj, bits, pot, res, grad_out, adj_out,
    wck, wadj, wbits, wpot, wres, zsend, zrecv, states, even, odd, adj_even, adj_odd, onsite, signs, rwin, weights,
    gbuf, gother, gall, obuf, xs, xr, zs, zr, vs, vr,
):
    x = lax.axis_index("row")
    z = lax.axis_index("col")
    y = lax.axis_index("vec")
    n_z = lax.axis_size("col")
    n_y = lax.axis_size("vec")
    across = {"row": 1 - x}
    right = {"col": lax.rem(z + 1, n_z)}
    left = {"col": lax.rem(z + n_z - 1, n_z)}
    peers = [{"vec": lax.rem(y + d, n_y)} for d in range(1, n_y)]

    barrier = pltpu.get_barrier_semaphore()
    for device in [across, right, left] + peers:
        pl.semaphore_signal(barrier, inc=1, device_id=device, device_id_type=MESH)
    pl.semaphore_wait(barrier, 3 + len(peers))

    def remote(source, target, send, recv, device):
        copy = pltpu.make_async_remote_copy(
            src_ref=source, dst_ref=target, send_sem=send, recv_sem=recv,
            device_id=device, device_id_type=MESH,
        )
        copy.start()
        return copy

    def to_x(source, target, index):
        return remote(source, target, xs.at[index], xr.at[index], across)

    theirs = pl.ds(2 * (1 - x), 2)
    mine = pl.ds(2 * x, 2)
    other = pl.ds(ROWS, ROWS)
    own = pl.ds(0, ROWS)
    c_ck = to_x(ck.at[:, :, theirs], wck.at[:, :, :, other], X_CK)
    c_adj = to_x(adj.at[:, theirs], wadj.at[:, :, other], X_ADJ)
    c_bits = to_x(bits.at[theirs], wbits.at[:, other], X_BITS)
    c_pot = to_x(pot, wpot.at[other], X_POT)
    c_res = to_x(res, wres.at[:, other], X_RES)

    wck[:, :, :, own] = ck[:, :, mine]
    wadj[:, :, own] = adj[:, mine]
    wbits[:, own] = bits[mine]
    wpot[own] = pot[...]
    wres[:, own] = res[...]

    lane = lax.broadcasted_iota(jnp.int32, (8, LANES), 1)

    def rows(j):
        return pl.ds(j, 8, stride=8)

    def pack(slot, j, planes):
        zsend[0, slot, j] = pick_quarter(lane, [turn(p, REACH * (q + 1)) for q, p in enumerate(planes)])
        zsend[1, slot, j] = pick_quarter(lane, [turn(p, REACH * q) for q, p in enumerate(planes)])

    def unpack(slot, j, q):
        from_left = turn(zrecv[0, slot, j], LANES - REACH - REACH * q)
        from_right = turn(zrecv[1, slot, j], LANES - REACH * q)
        return jnp.where(lane < 2 * REACH, from_right, from_left)

    def to_z(part):
        first, count = Z_PARTS[part]
        span = pl.ds(first, count)
        return [
            remote(zsend.at[d, span], zrecv.at[d, span], zs.at[d, part], zr.at[d, part], device)
            for d, device in enumerate((right, left))
        ]

    c_ck.wait()
    for j in range(DEPTH):
        for s in range(2):
            planes = [wck[s, k, v, rows(j)] for k in range(2) for v in range(2)]
            pack(s, j, planes)
            for q, plane in enumerate(planes):
                states[s * SEG + q // 2, q % 2, j] = plane
                (even, odd)[q // 2][s, q % 2, j, 0] = plane
    z_ck = to_z(Z_CK)

    pot_factor = scal[0]
    twice = scal[1]
    inv_count = scal[2]
    c_adj.wait()
    c_bits.wait()
    c_pot.wait()
    for j in range(DEPTH):
        planes = [wadj[k, v, rows(j)] for k in range(2) for v in range(2)]
        pack(2, j, planes)
        for q, plane in enumerate(planes):
            (adj_even, adj_odd)[q // 2][q % 2, j, 0] = plane
        sign = [(2 * wbits[v, rows(j)] - 1).astype(jnp.float32) * inv_count for v in range(2)]
        site = wpot[rows(j)].astype(jnp.float32) * pot_factor * twice
        pack(3, j, [sign[0], sign[1], site, site])
        signs[0, j, 0] = sign[0]
        signs[1, j, 0] = sign[1]
        onsite[j, 0] = site
    z_adj = to_z(Z_ADJ)

    c_res.wait()
    for j in range(DEPTH):
        for p in range(4):
            planes = [wres[4 * p + q, rows(j)] for q in range(4)]
            pack(4 + p, j, planes)
            for q, plane in enumerate(planes):
                rwin[j, 0, 4 * p + q] = plane
    z_res = to_z(Z_RES)

    def settle(copies):
        for copy in copies:
            copy.wait()

    settle(z_ck)
    for j in range(DEPTH):
        for s in range(2):
            for q in range(4):
                (even, odd)[q // 2][s, q % 2, j, 1] = unpack(s, j, q)
    settle(z_adj)
    for j in range(DEPTH):
        for q in range(4):
            (adj_even, adj_odd)[q // 2][q % 2, j, 1] = unpack(2, j, q)
        signs[0, j, 1] = unpack(3, j, 0)
        signs[1, j, 1] = unpack(3, j, 1)
        onsite[j, 1] = unpack(3, j, 2)

    first_lane = lane == 0
    last_lane = lane == LANES - 1

    def beside(ref, v, j):
        here = [ref[v, j, c] for c in range(2)]
        back = [pltpu.roll(w, 1, 1) for w in here]
        ahead = [pltpu.roll(w, LANES - 1, 1) for w in here]
        sums = []
        for c in range(2):
            before = jnp.where(first_lane, back[1 - c], back[c])
            after = jnp.where(last_lane, ahead[1 - c], ahead[c])
            if j == 0:
                above = pltpu.roll(ref[v, DEPTH - 1, c], 1, 0)
            else:
                above = ref[v, j - 1, c]
            if j == DEPTH - 1:
                below = pltpu.roll(ref[v, 0, c], 7, 0)
            else:
                below = ref[v, j + 1, c]
            sums.append((above + below) + (before + after))
        return here, sums

    def forward(half, carry):
        for step in range(2):
            now, then = (odd, even) if step == 0 else (even, odd)
            k = 2 + 2 * half + step
            for s in range(2):
                for v in range(2):
                    for j in range(DEPTH):
                        here, sums = beside(now.at[s], v, j)
                        for c in range(2):
                            value = (onsite[j, c] * here[c] - twice * sums[c]) - then[s, v, j, c]
                            then[s, v, j, c] = value
                            if c == 0:
                                states[s * SEG + k, v, j] = value
        return carry

    lax.fori_loop(0, SEG // 2 - 1, forward, 0)

    def halves(value):
        high = value.astype(jnp.bfloat16)
        return high, (value - high.astype(jnp.float32)).astype(jnp.bfloat16)

    def spread(value):
        pick_t = lax.broadcasted_iota(jnp.int32, (TERMS * 8, TERMS), 0) >> 3
        pick_t = pick_t == lax.broadcasted_iota(jnp.int32, (TERMS * 8, TERMS), 1)
        pick_e = lax.broadcasted_iota(jnp.int32, (ENERGIES, ENERGIES * 8), 1) >> 3
        pick_e = pick_e == lax.broadcasted_iota(jnp.int32, (ENERGIES, ENERGIES * 8), 0)
        same = lax.broadcasted_iota(jnp.int32, (TERMS * 8, ENERGIES * 8), 0)
        same = (same & 7) == (lax.broadcasted_iota(jnp.int32, (TERMS * 8, ENERGIES * 8), 1) & 7)
        flag = lambda mask: jnp.where(mask, 1.0, 0.0).astype(jnp.bfloat16)
        tall = jnp.dot(flag(pick_t), value, preferred_element_type=jnp.float32).astype(jnp.bfloat16)
        wide = jnp.dot(tall, flag(pick_e), preferred_element_type=jnp.float32)
        return jnp.where(same, wide, 0.0).astype(jnp.bfloat16)

    kron_high, kron_low = [spread(part) for part in halves(coefs[...])]

    def weigh(c):
        for j in range(DEPTH):
            high, low = halves(rwin[j, c].reshape(ENERGIES * 8, LANES))
            dot = lambda a, b: jnp.dot(a, b, preferred_element_type=jnp.float32)
            total = dot(kron_high, high) + (dot(kron_high, low) + dot(kron_low, high))
            weights[j, c] = total.reshape(TERMS, 8, LANES)

    weigh(0)
    settle(z_res)
    for j in range(DEPTH):
        for p in range(4):
            for q in range(4):
                rwin[j, 1, 4 * p + q] = unpack(4 + p, j, q)
    weigh(1)

    def adjoint(half, sums_in):
        grads = list(sums_in)
        for step in range(2):
            now, then = (adj_even, adj_odd) if step == 0 else (adj_odd, adj_even)
            t = TERMS - 1 - step - 2 * half
            for v in range(2):
                for j in range(DEPTH):
                    here, sums = beside(now, v, j)
                    grads[j] = grads[j] + here[0] * states[t, v, j]
                    for c in range(2):
                        source = weights[j, c, t] * signs[v, j, c]
                        then[v, j, c] = (source + onsite[j, c] * here[c]) - (twice * sums[c] + then[v, j, c])
        return tuple(grads)

    zero = jnp.zeros((8, LANES), jnp.float32)
    grads = lax.fori_loop(0, TERMS // 2, adjoint, (zero,) * DEPTH)

    for j in range(DEPTH):
        gbuf[rows(j)] = grads[j]
        for k in range(2):
            for v in range(2):
                obuf[k, v, rows(j)] = (adj_even, adj_odd)[k][v, j, 0]
    c_grad = to_x(gbuf.at[other], gother, X_GRAD)
    c_out = to_x(obuf.at[:, :, other], adj_out.at[:, mine], X_OUT)
    adj_out[:, mine] = obuf[:, :, own]
    c_grad.wait()
    gall[y] = gbuf[own] + gother[...]
    shares = [
        remote(gall.at[y], gall.at[y], vs.at[d], vr.at[d], device) for d, device in enumerate(peers)
    ]
    settle(shares)
    total = gall[0]
    for d in range(1, n_y):
        total = total + gall[d]
    grad_out[...] = total * twice
    c_out.wait()


def windowed(
    checkpoints,
    adjoints_in,
    vector_bits,
    potential_int,
    pot_scale,
    energies,
    residual,
    first_segment,
):
    n_y = lax.axis_size("vec")
    pot_factor = pot_scale[0]
    twice = 2.0 / (4.5 + QMAX * pot_factor)
    coefficients = window_coefs(first_segment, energies)
    inv_count = 1.0 / (n_y * vector_bits.shape[0])
    scal = jnp.stack([pot_factor, twice, jnp.float32(inv_count)])
    f32, i32 = jnp.float32, jnp.int32
    vmem = pl.BlockSpec(memory_space=pltpu.VMEM)
    tile = (8, LANES)
    gradient, adjoint_out = pl.pallas_call(
        kernel,
        out_shape=(
            jax.ShapeDtypeStruct(potential_int.shape, f32),
            jax.ShapeDtypeStruct(adjoints_in.shape, f32),
        ),
        in_specs=[pl.BlockSpec(memory_space=pltpu.SMEM)] + [vmem] * 6,
        out_specs=(vmem, vmem),
        scratch_shapes=[
            pltpu.VMEM((2, 2, 2, 2 * ROWS, LANES), f32),
            pltpu.VMEM((2, 2, 2 * ROWS, LANES), f32),
            pltpu.VMEM((2, 2 * ROWS, LANES), i32),
            pltpu.VMEM((2 * ROWS, LANES), i32),
            pltpu.VMEM((ENERGIES, 2 * ROWS, LANES), f32),
            pltpu.VMEM((2, PACKS, DEPTH) + tile, f32),
            pltpu.VMEM((2, PACKS, DEPTH) + tile, f32),
            pltpu.VMEM((TERMS, 2, DEPTH) + tile, f32),
            pltpu.VMEM((2, 2, DEPTH, 2) + tile, f32),
            pltpu.VMEM((2, 2, DEPTH, 2) + tile, f32),
            pltpu.VMEM((2, DEPTH, 2) + tile, f32),
            pltpu.VMEM((2, DEPTH, 2) + tile, f32),
            pltpu.VMEM((DEPTH, 2) + tile, f32),
            pltpu.VMEM((2, DEPTH, 2) + tile, f32),
            pltpu.VMEM((DEPTH, 2, ENERGIES) + tile, f32),
            pltpu.VMEM((DEPTH, 2, TERMS) + tile, f32),
            pltpu.VMEM((2 * ROWS, LANES), f32),
            pltpu.VMEM((ROWS, LANES), f32),
            pltpu.VMEM((n_y, ROWS, LANES), f32),
            pltpu.VMEM((2, 2, 2 * ROWS, LANES), f32),
            pltpu.SemaphoreType.DMA((7,)),
            pltpu.SemaphoreType.DMA((7,)),
            pltpu.SemaphoreType.DMA((2, 3)),
            pltpu.SemaphoreType.DMA((2, 3)),
            pltpu.SemaphoreType.DMA((n_y - 1,)),
            pltpu.SemaphoreType.DMA((n_y - 1,)),
        ],
        compiler_params=pltpu.CompilerParams(
            collective_id=0, has_side_effects=True, vmem_limit_bytes=40 * 1024 * 1024
        ),
    )(scal, coefficients, checkpoints, adjoints_in, vector_bits, potential_int, residual)
    return gradient, adjoint_out


def solution(mesh):
    fits = mesh.shape["row"] == 2 and mesh.shape["col"] > 2
    return jax.shard_map(
        windowed if fits else per_device,
        mesh=mesh,
        in_specs=(
            P(None, None, "vec", "row", "col"),
            P(None, "vec", "row", "col"),
            P("vec", "row", "col"),
            P("row", "col"),
            P(),
            P(),
            P(None, "row", "col"),
            P(),
        ),
        out_specs=(P("row", "col"), P(None, "vec", "row", "col")),
        check_vma=False,
    )
```

```python
import math

import jax
import jax.numpy as jnp
from jax import lax
from jax.experimental import pallas as pl
from jax.experimental.pallas import tpu as pltpu
from jax.sharding import PartitionSpec as P

SEG = 16
MOMENTS = 1024
QMAX = 32767


def extended_2(value, sides, width):
    for axis, dim in sides:
        devices, length = (lax.axis_size(axis), value.shape[dim])
        up = [(i, (i + 1) % devices) for i in range(devices)]
        down = [(j, i) for i, j in up]
        last = lax.slice_in_dim(value, length - width, length, axis=dim)
        initial = lax.slice_in_dim(value, 0, width, axis=dim)
        before = lax.ppermute(last, axis, up)
        after = lax.ppermute(initial, axis, down)
        value = jnp.concatenate([before, value, after], axis=dim)
    return value


def window_coefs(first_segment, energies):
    moment_order = first_segment[0] * SEG + jnp.arange(2 * SEG, dtype=jnp.int32)
    degree = moment_order.astype(jnp.float32)
    kernel_norm = float(MOMENTS + 1)
    angle_step = math.pi / kernel_norm
    jackson = (
        (kernel_norm - degree) * jnp.cos(angle_step * degree)
        + jnp.sin(angle_step * degree) * (math.cos(angle_step) / math.sin(angle_step))
    ) / kernel_norm
    factor = jnp.where(moment_order == 0, 1.0, 2.0).astype(jnp.float32)
    angles = jnp.arccos(energies)
    cosines = jnp.cos(degree[:, None] * angles[None, :])
    return (jackson * factor)[:, None] * cosines / (math.pi * jnp.sin(angles))[None, :]


def stencil(extended, onsite, inv_span):
    middle = extended[..., 1:-1, 1:-1]
    beside = (
        extended[..., 2:, 1:-1]
        + extended[..., :-2, 1:-1]
        + extended[..., 1:-1, 2:]
        + extended[..., 1:-1, :-2]
    )
    return inv_span * (onsite * middle - beside)


def per_device(
    checkpoints,
    adjoints_in,
    vector_bits,
    potential_int,
    pot_scale,
    energies,
    residual,
    first_segment,
):
    pot_factor = pot_scale[0]
    inv_span = 1.0 / (4.5 + QMAX * pot_factor)
    onsite = potential_int.astype(jnp.float32) * pot_factor
    coefficients = window_coefs(first_segment, energies)
    vector_count = lax.axis_size("vec") * vector_bits.shape[0]
    inv_count = 1.0 / vector_count
    sign_weights = (2 * vector_bits - 1).astype(jnp.float32) * inv_count
    earlier = checkpoints[:, 0]
    current = checkpoints[:, 1]
    zero_grad = jnp.zeros(onsite.shape, jnp.float32)
    carried = (adjoints_in[0], adjoints_in[1], zero_grad)
    weights = jnp.einsum("ne,eij->nij", coefficients, residual, precision=lax.Precision.HIGHEST)

    def forward_step(pair_state, unused):
        before, now = pair_state
        padded = extended_2(now, (("row", 2), ("col", 3)), 1)
        advanced = 2.0 * stencil(padded, onsite, inv_span) - before
        return ((now, advanced), advanced)

    _, generated = lax.scan(forward_step, (earlier, current), None, length=SEG - 2)
    states = jnp.concatenate([earlier[None], current[None], generated], axis=0)

    def adjoint_step(step_carry, inputs):
        after_one, after_two, accum_grad = step_carry
        state_now, weight_now = inputs
        padded = extended_2(after_one, (("row", 1), ("col", 2)), 1)
        accum_grad = accum_grad + jnp.sum(after_one * state_now, axis=0)
        advanced = weight_now * sign_weights + 2.0 * stencil(padded, onsite, inv_span) - after_two
        return ((advanced, after_one, accum_grad), None)

    for segment in (1, 0):
        carried, _ = lax.scan(
            adjoint_step,
            carried,
            (states[:, segment], weights[segment * SEG : (segment + 1) * SEG]),
            reverse=True,
        )
    adjoint_zero, adjoint_first, accum_grad = carried
    gradient = lax.psum(accum_grad, "vec") * (2.0 * inv_span)
    return (gradient, jnp.stack([adjoint_zero, adjoint_first]))


MESH = pl.DeviceIdType.MESH
TERMS = 2 * SEG
ROWS = 32
LANES = 128
REACH = 32
DEPTH = 8
ENERGIES = 16
X_CK, X_ADJ, X_BITS, X_POT, X_RES, X_GRAD, X_OUT = range(7)
Z_CK, Z_ADJ, Z_RES = range(3)
V_ROWS, V_HALO, V_GRAD = range(3)
QUARTER = 4


def pick(lane, parts):
    width = LANES // len(parts)
    while len(parts) > 1:
        parts = [jnp.where((lane & width) == 0, low, high) for low, high in zip(parts[::2], parts[1::2])]
        width = 2 * width
    return parts[0]


def turn(value, shift):
    shift = shift % LANES
    return value if shift == 0 else pltpu.roll(value, shift, 1)


def kernel(
    scal, coefs, ck, adj, bits, pot, res, grad_out, adj_out,
    wck, wadj, wbits, wpot, wres, zsend, zrecv, zres, states, even, odd, adj_even, adj_odd, onsite, signs, rwin, weights,
    gbuf, gother, gall, obuf, xs, xr, zs, zr, vs, vr,
):
    x = lax.axis_index("row")
    z = lax.axis_index("col")
    y = lax.axis_index("vec")
    n_z = lax.axis_size("col")
    n_y = lax.axis_size("vec")
    across = {"row": 1 - x}
    right = {"col": lax.rem(z + 1, n_z)}
    left = {"col": lax.rem(z + n_z - 1, n_z)}
    peers = [{"vec": lax.rem(y + d, n_y)} for d in range(1, n_y)]

    barrier = pltpu.get_barrier_semaphore()
    for device in [across, right, left] + peers:
        pl.semaphore_signal(barrier, inc=1, device_id=device, device_id_type=MESH)
    pl.semaphore_wait(barrier, 3 + len(peers))

    def remote(source, target, send, recv, device):
        copy = pltpu.make_async_remote_copy(
            src_ref=source, dst_ref=target, send_sem=send, recv_sem=recv,
            device_id=device, device_id_type=MESH,
        )
        copy.start()
        return copy

    def to_x(source, target, index):
        return remote(source, target, xs.at[index], xr.at[index], across)

    theirs = pl.ds(2 * (1 - x), 2)
    mine = pl.ds(2 * x, 2)
    other = pl.ds(ROWS, ROWS)
    own = pl.ds(0, ROWS)
    share = pl.ds(QUARTER * y, QUARTER)
    c_res = to_x(res.at[share], wres.at[share, other], X_RES)
    c_ck = to_x(ck.at[:, :, theirs], wck.at[:, :, :, other], X_CK)
    c_adj = to_x(adj.at[:, theirs], wadj.at[:, :, other], X_ADJ)
    c_bits = to_x(bits.at[theirs], wbits.at[:, other], X_BITS)
    c_pot = to_x(pot, wpot.at[other], X_POT)

    wck[:, :, :, own] = ck[:, :, mine]
    wadj[:, :, own] = adj[:, mine]
    wbits[:, own] = bits[mine]
    wpot[own] = pot[...]
    wres[:, own] = res[...]

    lane = lax.broadcasted_iota(jnp.int32, (8, LANES), 1)

    def rows(j):
        return pl.ds(j, 8, stride=8)

    def pack(slot, j, planes):
        width = LANES // len(planes)
        zsend[0, slot, j] = pick(lane, [turn(p, width * (q + 1)) for q, p in enumerate(planes)])
        zsend[1, slot, j] = pick(lane, [turn(p, width * q) for q, p in enumerate(planes)])

    def unpack(pair, q, count):
        width = LANES // count
        from_left = turn(pair[0], LANES - width - width * q)
        from_right = turn(pair[1], LANES - width * q)
        return jnp.where(lane < LANES // 2, from_right, from_left)

    def to_z(part, source, target):
        return [
            remote(source.at[d], target.at[d], zs.at[d, part], zr.at[d, part], device)
            for d, device in enumerate((right, left))
        ]

    def to_peers(part, ref):
        return [
            remote(ref, ref, vs.at[part, d], vr.at[part, d], device) for d, device in enumerate(peers)
        ]

    def settle(copies):
        for copy in copies:
            copy.wait()

    c_res.wait()
    g_rows = to_peers(V_ROWS, wres.at[share, other])
    for j in range(DEPTH):
        pack(3, j, [wres[QUARTER * y + q, rows(j)] for q in range(QUARTER)])
    z_res = to_z(Z_RES, zsend.at[:, 3], zres.at[:, y])

    c_ck.wait()
    for j in range(DEPTH):
        planes = [wck[s, k, v, rows(j)] for s in range(2) for k in range(2) for v in range(2)]
        pack(0, j, planes)
        for q, plane in enumerate(planes):
            s, k, v = q // 4, q // 2 % 2, q % 2
            states[s * SEG + k, v, j] = plane
            (even, odd)[k][s, v, j, 0] = plane
    z_ck = to_z(Z_CK, zsend.at[:, pl.ds(0, 1)], zrecv.at[:, pl.ds(0, 1)])

    pot_factor = scal[0]
    twice = scal[1]
    inv_count = scal[2]
    c_adj.wait()
    c_bits.wait()
    c_pot.wait()
    for j in range(DEPTH):
        planes = [wadj[k, v, rows(j)] for k in range(2) for v in range(2)]
        pack(1, j, planes)
        for q, plane in enumerate(planes):
            (adj_even, adj_odd)[q // 2][q % 2, j, 0] = plane
        sign = [(2 * wbits[v, rows(j)] - 1).astype(jnp.float32) * inv_count for v in range(2)]
        site = wpot[rows(j)].astype(jnp.float32) * pot_factor * twice
        pack(2, j, [sign[0], sign[1], site, site])
        signs[0, j, 0] = sign[0]
        signs[1, j, 0] = sign[1]
        onsite[j, 0] = site
    z_adj = to_z(Z_ADJ, zsend.at[:, pl.ds(1, 2)], zrecv.at[:, pl.ds(1, 2)])

    settle(z_res)
    g_halo = to_peers(V_HALO, zres.at[:, y])

    def halves(value):
        high = value.astype(jnp.bfloat16)
        return high, (value - high.astype(jnp.float32)).astype(jnp.bfloat16)

    def spread(value):
        pick_t = lax.broadcasted_iota(jnp.int32, (TERMS * 8, TERMS), 0) >> 3
        pick_t = pick_t == lax.broadcasted_iota(jnp.int32, (TERMS * 8, TERMS), 1)
        pick_e = lax.broadcasted_iota(jnp.int32, (ENERGIES, ENERGIES * 8), 1) >> 3
        pick_e = pick_e == lax.broadcasted_iota(jnp.int32, (ENERGIES, ENERGIES * 8), 0)
        same = lax.broadcasted_iota(jnp.int32, (TERMS * 8, ENERGIES * 8), 0)
        same = (same & 7) == (lax.broadcasted_iota(jnp.int32, (TERMS * 8, ENERGIES * 8), 1) & 7)
        flag = lambda mask: jnp.where(mask, 1.0, 0.0).astype(jnp.bfloat16)
        tall = jnp.dot(flag(pick_t), value, preferred_element_type=jnp.float32).astype(jnp.bfloat16)
        wide = jnp.dot(tall, flag(pick_e), preferred_element_type=jnp.float32)
        return jnp.where(same, wide, 0.0).astype(jnp.bfloat16)

    kron_high, kron_low = [spread(part) for part in halves(coefs[...])]

    kron_wide = jnp.concatenate([kron_high, kron_high], axis=1)

    def weigh(c):
        for j in range(0, DEPTH, 2):
            block = [rwin[j + i, c].reshape(ENERGIES * 8, LANES) for i in range(2)]
            high, low = halves(jnp.concatenate(block, axis=1))
            total = jnp.dot(kron_wide, jnp.concatenate([high, low], axis=0), preferred_element_type=jnp.float32)
            total = total + jnp.dot(kron_low, high, preferred_element_type=jnp.float32)
            for i in range(2):
                weights[j + i, c] = total[:, i * LANES : (i + 1) * LANES].reshape(TERMS, 8, LANES)

    settle(g_rows)
    for j in range(DEPTH):
        for e in range(ENERGIES):
            rwin[j, 0, e] = wres[e, rows(j)]
    weigh(0)

    settle(z_ck)
    for j in range(DEPTH):
        pair = [zrecv[d, 0, j] for d in range(2)]
        for q in range(8):
            s, k, v = q // 4, q // 2 % 2, q % 2
            (even, odd)[k][s, v, j, 1] = unpack(pair, q, 8)
    settle(z_adj)
    for j in range(DEPTH):
        pair = [zrecv[d, 1, j] for d in range(2)]
        for q in range(4):
            (adj_even, adj_odd)[q // 2][q % 2, j, 1] = unpack(pair, q, 4)
        pair = [zrecv[d, 2, j] for d in range(2)]
        signs[0, j, 1] = unpack(pair, 0, 4)
        signs[1, j, 1] = unpack(pair, 1, 4)
        onsite[j, 1] = unpack(pair, 2, 4)

    first_lane = lane == 0
    last_lane = lane == LANES - 1

    def beside(ref, v, j):
        here = [ref[v, j, c] for c in range(2)]
        back = [pltpu.roll(w, 1, 1) for w in here]
        ahead = [pltpu.roll(w, LANES - 1, 1) for w in here]
        sums = []
        for c in range(2):
            before = jnp.where(first_lane, back[1 - c], back[c])
            after = jnp.where(last_lane, ahead[1 - c], ahead[c])
            if j == 0:
                above = pltpu.roll(ref[v, DEPTH - 1, c], 1, 0)
            else:
                above = ref[v, j - 1, c]
            if j == DEPTH - 1:
                below = pltpu.roll(ref[v, 0, c], 7, 0)
            else:
                below = ref[v, j + 1, c]
            sums.append((above + below) + (before + after))
        return here, sums

    def forward(half, carry):
        for step in range(2):
            now, then = (odd, even) if step == 0 else (even, odd)
            k = 2 + 2 * half + step
            for s in range(2):
                for v in range(2):
                    for j in range(DEPTH):
                        here, sums = beside(now.at[s], v, j)
                        for c in range(2):
                            value = (onsite[j, c] * here[c] - twice * sums[c]) - then[s, v, j, c]
                            then[s, v, j, c] = value
                            if c == 0:
                                states[s * SEG + k, v, j] = value
        return carry

    lax.fori_loop(0, SEG // 2 - 1, forward, 0)

    settle(g_halo)
    for j in range(DEPTH):
        for e in range(ENERGIES):
            pair = [zres[d, e // QUARTER, j] for d in range(2)]
            rwin[j, 1, e] = unpack(pair, e % QUARTER, QUARTER)
    weigh(1)

    def adjoint(half, sums_in):
        grads = list(sums_in)
        for step in range(2):
            now, then = (adj_even, adj_odd) if step == 0 else (adj_odd, adj_even)
            t = TERMS - 1 - step - 2 * half
            for v in range(2):
                for j in range(DEPTH):
                    here, sums = beside(now, v, j)
                    grads[j] = grads[j] + here[0] * states[t, v, j]
                    for c in range(2):
                        source = weights[j, c, t] * signs[v, j, c]
                        then[v, j, c] = (source + onsite[j, c] * here[c]) - (twice * sums[c] + then[v, j, c])
        return tuple(grads)

    zero = jnp.zeros((8, LANES), jnp.float32)
    grads = lax.fori_loop(0, TERMS // 2, adjoint, (zero,) * DEPTH)

    for j in range(DEPTH):
        gbuf[rows(j)] = grads[j]
        for k in range(2):
            for v in range(2):
                obuf[k, v, rows(j)] = (adj_even, adj_odd)[k][v, j, 0]
    c_grad = to_x(gbuf.at[other], gother, X_GRAD)
    c_out = to_x(obuf.at[:, :, other], adj_out.at[:, mine], X_OUT)
    adj_out[:, mine] = obuf[:, :, own]
    c_grad.wait()
    gall[y] = gbuf[own] + gother[...]
    settle(to_peers(V_GRAD, gall.at[y]))
    total = gall[0]
    for d in range(1, n_y):
        total = total + gall[d]
    grad_out[...] = total * twice
    c_out.wait()


def windowed(
    checkpoints,
    adjoints_in,
    vector_bits,
    potential_int,
    pot_scale,
    energies,
    residual,
    first_segment,
):
    n_y = lax.axis_size("vec")
    pot_factor = pot_scale[0]
    twice = 2.0 / (4.5 + QMAX * pot_factor)
    coefficients = window_coefs(first_segment, energies)
    inv_count = 1.0 / (n_y * vector_bits.shape[0])
    scal = jnp.stack([pot_factor, twice, jnp.float32(inv_count)])
    f32, i32 = jnp.float32, jnp.int32
    vmem = pl.BlockSpec(memory_space=pltpu.VMEM)
    tile = (8, LANES)
    gradient, adjoint_out = pl.pallas_call(
        kernel,
        out_shape=(
            jax.ShapeDtypeStruct(potential_int.shape, f32),
            jax.ShapeDtypeStruct(adjoints_in.shape, f32),
        ),
        in_specs=[pl.BlockSpec(memory_space=pltpu.SMEM)] + [vmem] * 6,
        out_specs=(vmem, vmem),
        scratch_shapes=[
            pltpu.VMEM((2, 2, 2, 2 * ROWS, LANES), f32),
            pltpu.VMEM((2, 2, 2 * ROWS, LANES), f32),
            pltpu.VMEM((2, 2 * ROWS, LANES), i32),
            pltpu.VMEM((2 * ROWS, LANES), i32),
            pltpu.VMEM((ENERGIES, 2 * ROWS, LANES), f32),
            pltpu.VMEM((2, 4, DEPTH) + tile, f32),
            pltpu.VMEM((2, 3, DEPTH) + tile, f32),
            pltpu.VMEM((2, n_y, DEPTH) + tile, f32),
            pltpu.VMEM((TERMS, 2, DEPTH) + tile, f32),
            pltpu.VMEM((2, 2, DEPTH, 2) + tile, f32),
            pltpu.VMEM((2, 2, DEPTH, 2) + tile, f32),
            pltpu.VMEM((2, DEPTH, 2) + tile, f32),
            pltpu.VMEM((2, DEPTH, 2) + tile, f32),
            pltpu.VMEM((DEPTH, 2) + tile, f32),
            pltpu.VMEM((2, DEPTH, 2) + tile, f32),
            pltpu.VMEM((DEPTH, 2, ENERGIES) + tile, f32),
            pltpu.VMEM((DEPTH, 2, TERMS) + tile, f32),
            pltpu.VMEM((2 * ROWS, LANES), f32),
            pltpu.VMEM((ROWS, LANES), f32),
            pltpu.VMEM((n_y, ROWS, LANES), f32),
            pltpu.VMEM((2, 2, 2 * ROWS, LANES), f32),
            pltpu.SemaphoreType.DMA((7,)),
            pltpu.SemaphoreType.DMA((7,)),
            pltpu.SemaphoreType.DMA((2, 3)),
            pltpu.SemaphoreType.DMA((2, 3)),
            pltpu.SemaphoreType.DMA((3, n_y - 1)),
            pltpu.SemaphoreType.DMA((3, n_y - 1)),
        ],
        compiler_params=pltpu.CompilerParams(
            collective_id=0, has_side_effects=True, vmem_limit_bytes=40 * 1024 * 1024
        ),
    )(scal, coefficients, checkpoints, adjoints_in, vector_bits, potential_int, residual)
    return gradient, adjoint_out


def solution(mesh):
    fits = mesh.shape["row"] == 2 and mesh.shape["col"] > 2 and mesh.shape["vec"] == 4
    return jax.shard_map(
        windowed if fits else per_device,
        mesh=mesh,
        in_specs=(
            P(None, None, "vec", "row", "col"),
            P(None, "vec", "row", "col"),
            P("vec", "row", "col"),
            P("row", "col"),
            P(),
            P(),
            P(None, "row", "col"),
            P(),
        ),
        out_specs=(P("row", "col"), P(None, "vec", "row", "col")),
        check_vma=False,
    )
```

```python
import math

import jax
import jax.numpy as jnp
from jax import lax
from jax.experimental import pallas as pl
from jax.experimental.pallas import tpu as pltpu
from jax.sharding import PartitionSpec as P

SEG = 16
MOMENTS = 1024
QMAX = 32767


def extended_2(value, sides, width):
    for axis, dim in sides:
        devices, length = (lax.axis_size(axis), value.shape[dim])
        up = [(i, (i + 1) % devices) for i in range(devices)]
        down = [(j, i) for i, j in up]
        last = lax.slice_in_dim(value, length - width, length, axis=dim)
        initial = lax.slice_in_dim(value, 0, width, axis=dim)
        before = lax.ppermute(last, axis, up)
        after = lax.ppermute(initial, axis, down)
        value = jnp.concatenate([before, value, after], axis=dim)
    return value


def window_coefs(first_segment, energies):
    moment_order = first_segment[0] * SEG + jnp.arange(2 * SEG, dtype=jnp.int32)
    degree = moment_order.astype(jnp.float32)
    kernel_norm = float(MOMENTS + 1)
    angle_step = math.pi / kernel_norm
    jackson = (
        (kernel_norm - degree) * jnp.cos(angle_step * degree)
        + jnp.sin(angle_step * degree) * (math.cos(angle_step) / math.sin(angle_step))
    ) / kernel_norm
    factor = jnp.where(moment_order == 0, 1.0, 2.0).astype(jnp.float32)
    angles = jnp.arccos(energies)
    cosines = jnp.cos(degree[:, None] * angles[None, :])
    return (jackson * factor)[:, None] * cosines / (math.pi * jnp.sin(angles))[None, :]


def stencil(extended, onsite, inv_span):
    middle = extended[..., 1:-1, 1:-1]
    beside = (
        extended[..., 2:, 1:-1]
        + extended[..., :-2, 1:-1]
        + extended[..., 1:-1, 2:]
        + extended[..., 1:-1, :-2]
    )
    return inv_span * (onsite * middle - beside)


def per_device(
    checkpoints,
    adjoints_in,
    vector_bits,
    potential_int,
    pot_scale,
    energies,
    residual,
    first_segment,
):
    pot_factor = pot_scale[0]
    inv_span = 1.0 / (4.5 + QMAX * pot_factor)
    onsite = potential_int.astype(jnp.float32) * pot_factor
    coefficients = window_coefs(first_segment, energies)
    vector_count = lax.axis_size("vec") * vector_bits.shape[0]
    inv_count = 1.0 / vector_count
    sign_weights = (2 * vector_bits - 1).astype(jnp.float32) * inv_count
    earlier = checkpoints[:, 0]
    current = checkpoints[:, 1]
    zero_grad = jnp.zeros(onsite.shape, jnp.float32)
    carried = (adjoints_in[0], adjoints_in[1], zero_grad)
    weights = jnp.einsum("ne,eij->nij", coefficients, residual, precision=lax.Precision.HIGHEST)

    def forward_step(pair_state, unused):
        before, now = pair_state
        padded = extended_2(now, (("row", 2), ("col", 3)), 1)
        advanced = 2.0 * stencil(padded, onsite, inv_span) - before
        return ((now, advanced), advanced)

    _, generated = lax.scan(forward_step, (earlier, current), None, length=SEG - 2)
    states = jnp.concatenate([earlier[None], current[None], generated], axis=0)

    def adjoint_step(step_carry, inputs):
        after_one, after_two, accum_grad = step_carry
        state_now, weight_now = inputs
        padded = extended_2(after_one, (("row", 1), ("col", 2)), 1)
        accum_grad = accum_grad + jnp.sum(after_one * state_now, axis=0)
        advanced = weight_now * sign_weights + 2.0 * stencil(padded, onsite, inv_span) - after_two
        return ((advanced, after_one, accum_grad), None)

    for segment in (1, 0):
        carried, _ = lax.scan(
            adjoint_step,
            carried,
            (states[:, segment], weights[segment * SEG : (segment + 1) * SEG]),
            reverse=True,
        )
    adjoint_zero, adjoint_first, accum_grad = carried
    gradient = lax.psum(accum_grad, "vec") * (2.0 * inv_span)
    return (gradient, jnp.stack([adjoint_zero, adjoint_first]))


MESH = pl.DeviceIdType.MESH
TERMS = 2 * SEG
ROWS = 32
LANES = 128
REACH = 32
DEPTH = 8
ENERGIES = 16
X_CK, X_ADJ, X_BITS, X_POT, X_RES, X_OUT = range(6)
Z_CK, Z_ADJ, Z_RES = range(3)
V_ROWS, V_HALO, V_GRAD, V_CROSS = range(4)
QUARTER = 4


def pick(lane, parts):
    width = LANES // len(parts)
    while len(parts) > 1:
        parts = [jnp.where((lane & width) == 0, low, high) for low, high in zip(parts[::2], parts[1::2])]
        width = 2 * width
    return parts[0]


def turn(value, shift):
    shift = shift % LANES
    return value if shift == 0 else pltpu.roll(value, shift, 1)


def kernel(
    scal, coefs, ck, adj, bits, pot, res, grad_out, adj_out,
    wck, wadj, wbits, wpot, wres, zsend, zrecv, zres, states, even, odd, adj_even, adj_odd, onsite, signs, rwin, weights,
    gbuf, gall, obuf, ls, xs, xr, zs, zr, vs, vr,
):
    x = lax.axis_index("row")
    z = lax.axis_index("col")
    y = lax.axis_index("vec")
    n_z = lax.axis_size("col")
    n_y = lax.axis_size("vec")
    across = {"row": 1 - x}
    right = {"col": lax.rem(z + 1, n_z)}
    left = {"col": lax.rem(z + n_z - 1, n_z)}
    peers = [{"vec": lax.rem(y + d, n_y)} for d in range(1, n_y)]
    far = [{"row": 1 - x, "vec": lax.rem(y + d, n_y)} for d in range(n_y)]

    barrier = pltpu.get_barrier_semaphore()
    for device in [right, left] + peers + far:
        pl.semaphore_signal(barrier, inc=1, device_id=device, device_id_type=MESH)
    pl.semaphore_wait(barrier, 2 + len(peers) + len(far))

    def remote(source, target, send, recv, device):
        copy = pltpu.make_async_remote_copy(
            src_ref=source, dst_ref=target, send_sem=send, recv_sem=recv,
            device_id=device, device_id_type=MESH,
        )
        copy.start()
        return copy

    def to_x(source, target, index):
        return remote(source, target, xs.at[index], xr.at[index], across)

    theirs = pl.ds(2 * (1 - x), 2)
    mine = pl.ds(2 * x, 2)
    other = pl.ds(ROWS, ROWS)
    own = pl.ds(0, ROWS)
    share = pl.ds(QUARTER * y, QUARTER)
    c_res = to_x(res.at[share], wres.at[share, other], X_RES)
    c_ck = to_x(ck.at[:, :, theirs], wck.at[:, :, :, other], X_CK)
    c_adj = to_x(adj.at[:, theirs], wadj.at[:, :, other], X_ADJ)
    c_bits = to_x(bits.at[theirs], wbits.at[:, other], X_BITS)
    c_pot = to_x(pot, wpot.at[other], X_POT)

    def local(source, target, index):
        copy = pltpu.make_async_copy(source, target, ls.at[index])
        copy.start()
        return copy

    l_res = local(res, wres.at[:, own], X_RES)
    l_ck = local(ck.at[:, :, mine], wck.at[:, :, :, own], X_CK)
    l_adj = local(adj.at[:, mine], wadj.at[:, :, own], X_ADJ)
    l_bits = local(bits.at[mine], wbits.at[:, own], X_BITS)
    l_pot = local(pot, wpot.at[own], X_POT)

    lane = lax.broadcasted_iota(jnp.int32, (8, LANES), 1)

    def rows(j):
        return pl.ds(j, 8, stride=8)

    def pack(slot, j, planes):
        width = LANES // len(planes)
        zsend[0, slot, j] = pick(lane, [turn(p, width * (q + 1)) for q, p in enumerate(planes)])
        zsend[1, slot, j] = pick(lane, [turn(p, width * q) for q, p in enumerate(planes)])

    def unpack(pair, q, count):
        width = LANES // count
        from_left = turn(pair[0], LANES - width - width * q)
        from_right = turn(pair[1], LANES - width * q)
        return jnp.where(lane < LANES // 2, from_right, from_left)

    def to_z(part, source, target):
        return [
            remote(source.at[d], target.at[d], zs.at[d, part], zr.at[d, part], device)
            for d, device in enumerate((right, left))
        ]

    def fan(part, source, target, devices):
        return [
            remote(source, target, vs.at[part, d], vr.at[part, d], device) for d, device in enumerate(devices)
        ]

    def to_peers(part, ref):
        return fan(part, ref, ref, peers)

    def settle(copies):
        for copy in copies:
            copy.wait()

    l_res.wait()
    c_res.wait()
    g_rows = to_peers(V_ROWS, wres.at[share, other])
    for j in range(DEPTH):
        pack(3, j, [wres[QUARTER * y + q, rows(j)] for q in range(QUARTER)])
    z_res = to_z(Z_RES, zsend.at[:, 3], zres.at[:, y])

    l_ck.wait()
    c_ck.wait()
    for j in range(DEPTH):
        planes = [wck[s, k, v, rows(j)] for s in range(2) for k in range(2) for v in range(2)]
        pack(0, j, planes)
        for q, plane in enumerate(planes):
            s, k, v = q // 4, q // 2 % 2, q % 2
            states[s * SEG + k, v, j] = plane
            (even, odd)[k][s, v, j, 0] = plane
    z_ck = to_z(Z_CK, zsend.at[:, pl.ds(0, 1)], zrecv.at[:, pl.ds(0, 1)])

    pot_factor = scal[0]
    twice = scal[1]
    inv_count = scal[2]
    settle([l_adj, l_bits, l_pot])
    c_adj.wait()
    c_bits.wait()
    c_pot.wait()
    for j in range(DEPTH):
        planes = [wadj[k, v, rows(j)] for k in range(2) for v in range(2)]
        pack(1, j, planes)
        for q, plane in enumerate(planes):
            (adj_even, adj_odd)[q // 2][q % 2, j, 0] = plane
        sign = [(2 * wbits[v, rows(j)] - 1).astype(jnp.float32) * inv_count for v in range(2)]
        site = wpot[rows(j)].astype(jnp.float32) * pot_factor * twice
        pack(2, j, [sign[0], sign[1], site, site])
        signs[0, j, 0] = sign[0]
        signs[1, j, 0] = sign[1]
        onsite[j, 0] = site
    z_adj = to_z(Z_ADJ, zsend.at[:, pl.ds(1, 2)], zrecv.at[:, pl.ds(1, 2)])

    settle(z_res)
    g_halo = to_peers(V_HALO, zres.at[:, y])

    def halves(value):
        high = value.astype(jnp.bfloat16)
        return high, (value - high.astype(jnp.float32)).astype(jnp.bfloat16)

    def spread(value):
        pick_t = lax.broadcasted_iota(jnp.int32, (TERMS * 8, TERMS), 0) >> 3
        pick_t = pick_t == lax.broadcasted_iota(jnp.int32, (TERMS * 8, TERMS), 1)
        pick_e = lax.broadcasted_iota(jnp.int32, (ENERGIES, ENERGIES * 8), 1) >> 3
        pick_e = pick_e == lax.broadcasted_iota(jnp.int32, (ENERGIES, ENERGIES * 8), 0)
        same = lax.broadcasted_iota(jnp.int32, (TERMS * 8, ENERGIES * 8), 0)
        same = (same & 7) == (lax.broadcasted_iota(jnp.int32, (TERMS * 8, ENERGIES * 8), 1) & 7)
        flag = lambda mask: jnp.where(mask, 1.0, 0.0).astype(jnp.bfloat16)
        tall = jnp.dot(flag(pick_t), value, preferred_element_type=jnp.float32).astype(jnp.bfloat16)
        wide = jnp.dot(tall, flag(pick_e), preferred_element_type=jnp.float32)
        return jnp.where(same, wide, 0.0).astype(jnp.bfloat16)

    kron_high, kron_low = [spread(part) for part in halves(coefs[...])]

    kron_wide = jnp.concatenate([kron_high, kron_high], axis=1)

    def weigh(c):
        for j in range(0, DEPTH, 2):
            block = [rwin[j + i, c].reshape(ENERGIES * 8, LANES) for i in range(2)]
            high, low = halves(jnp.concatenate(block, axis=1))
            total = jnp.dot(kron_wide, jnp.concatenate([high, low], axis=0), preferred_element_type=jnp.float32)
            total = total + jnp.dot(kron_low, high, preferred_element_type=jnp.float32)
            for i in range(2):
                weights[j + i, c] = total[:, i * LANES : (i + 1) * LANES].reshape(TERMS, 8, LANES)

    settle(g_rows)
    for j in range(DEPTH):
        for e in range(ENERGIES):
            rwin[j, 0, e] = wres[e, rows(j)]
    weigh(0)

    settle(z_ck)
    for j in range(DEPTH):
        pair = [zrecv[d, 0, j] for d in range(2)]
        for q in range(8):
            s, k, v = q // 4, q // 2 % 2, q % 2
            (even, odd)[k][s, v, j, 1] = unpack(pair, q, 8)
    settle(z_adj)
    for j in range(DEPTH):
        pair = [zrecv[d, 1, j] for d in range(2)]
        for q in range(4):
            (adj_even, adj_odd)[q // 2][q % 2, j, 1] = unpack(pair, q, 4)
        pair = [zrecv[d, 2, j] for d in range(2)]
        signs[0, j, 1] = unpack(pair, 0, 4)
        signs[1, j, 1] = unpack(pair, 1, 4)
        onsite[j, 1] = unpack(pair, 2, 4)

    first_lane = lane == 0
    last_lane = lane == LANES - 1

    def beside(ref, v, j):
        here = [ref[v, j, c] for c in range(2)]
        back = [pltpu.roll(w, 1, 1) for w in here]
        ahead = [pltpu.roll(w, LANES - 1, 1) for w in here]
        sums = []
        for c in range(2):
            before = jnp.where(first_lane, back[1 - c], back[c])
            after = jnp.where(last_lane, ahead[1 - c], ahead[c])
            if j == 0:
                above = pltpu.roll(ref[v, DEPTH - 1, c], 1, 0)
            else:
                above = ref[v, j - 1, c]
            if j == DEPTH - 1:
                below = pltpu.roll(ref[v, 0, c], 7, 0)
            else:
                below = ref[v, j + 1, c]
            sums.append((above + below) + (before + after))
        return here, sums

    def forward(half, carry):
        for step in range(2):
            now, then = (odd, even) if step == 0 else (even, odd)
            k = 2 + 2 * half + step
            for s in range(2):
                for v in range(2):
                    for j in range(DEPTH):
                        here, sums = beside(now.at[s], v, j)
                        for c in range(2):
                            value = (onsite[j, c] * here[c] - twice * sums[c]) - then[s, v, j, c]
                            then[s, v, j, c] = value
                            if c == 0:
                                states[s * SEG + k, v, j] = value
        return carry

    lax.fori_loop(0, SEG // 2 - 1, forward, 0)

    settle(g_halo)
    for j in range(DEPTH):
        for e in range(ENERGIES):
            pair = [zres[d, e // QUARTER, j] for d in range(2)]
            rwin[j, 1, e] = unpack(pair, e % QUARTER, QUARTER)
    weigh(1)

    def adjoint(half, sums_in):
        grads = list(sums_in)
        for step in range(2):
            now, then = (adj_even, adj_odd) if step == 0 else (adj_odd, adj_even)
            t = TERMS - 1 - step - 2 * half
            for v in range(2):
                for j in range(DEPTH):
                    here, sums = beside(now, v, j)
                    grads[j] = grads[j] + here[0] * states[t, v, j]
                    for c in range(2):
                        source = weights[j, c, t] * signs[v, j, c]
                        then[v, j, c] = (source + onsite[j, c] * here[c]) - (twice * sums[c] + then[v, j, c])
        return tuple(grads)

    zero = jnp.zeros((8, LANES), jnp.float32)
    grads = lax.fori_loop(0, TERMS // 2, adjoint, (zero,) * DEPTH)

    for j in range(DEPTH):
        gbuf[rows(j)] = grads[j]
        for k in range(2):
            for v in range(2):
                obuf[k, v, rows(j)] = (adj_even, adj_odd)[k][v, j, 0]
    sums = fan(V_CROSS, gbuf.at[other], gall.at[x, y], far)
    gall[x, y] = gbuf[own]
    sums += to_peers(V_GRAD, gall.at[x, y])
    c_out = to_x(obuf.at[:, :, other], adj_out.at[:, mine], X_OUT)
    l_out = local(obuf.at[:, :, own], adj_out.at[:, mine], X_OUT)
    settle(sums)
    total = gall[0, 0] + gall[1, 0]
    for d in range(1, n_y):
        total = total + (gall[0, d] + gall[1, d])
    gbuf[own] = total * twice
    l_grad = local(gbuf.at[own], grad_out, X_CK)
    l_out.wait()
    c_out.wait()
    l_grad.wait()


def windowed(
    checkpoints,
    adjoints_in,
    vector_bits,
    potential_int,
    pot_scale,
    energies,
    residual,
    first_segment,
):
    n_y = lax.axis_size("vec")
    pot_factor = pot_scale[0]
    twice = 2.0 / (4.5 + QMAX * pot_factor)
    coefficients = window_coefs(first_segment, energies)
    inv_count = 1.0 / (n_y * vector_bits.shape[0])
    scal = jnp.stack([pot_factor, twice, jnp.float32(inv_count)])
    f32, i32 = jnp.float32, jnp.int32
    vmem = pl.BlockSpec(memory_space=pltpu.VMEM)
    tile = (8, LANES)
    gradient, adjoint_out = pl.pallas_call(
        kernel,
        out_shape=(
            jax.ShapeDtypeStruct(potential_int.shape, f32),
            jax.ShapeDtypeStruct(adjoints_in.shape, f32),
        ),
        in_specs=[pl.BlockSpec(memory_space=pltpu.SMEM), vmem] + [pl.BlockSpec(memory_space=pl.ANY)] * 5,
        out_specs=(pl.BlockSpec(memory_space=pl.ANY),) * 2,
        scratch_shapes=[
            pltpu.VMEM((2, 2, 2, 2 * ROWS, LANES), f32),
            pltpu.VMEM((2, 2, 2 * ROWS, LANES), f32),
            pltpu.VMEM((2, 2 * ROWS, LANES), i32),
            pltpu.VMEM((2 * ROWS, LANES), i32),
            pltpu.VMEM((ENERGIES, 2 * ROWS, LANES), f32),
            pltpu.VMEM((2, 4, DEPTH) + tile, f32),
            pltpu.VMEM((2, 3, DEPTH) + tile, f32),
            pltpu.VMEM((2, n_y, DEPTH) + tile, f32),
            pltpu.VMEM((TERMS, 2, DEPTH) + tile, f32),
            pltpu.VMEM((2, 2, DEPTH, 2) + tile, f32),
            pltpu.VMEM((2, 2, DEPTH, 2) + tile, f32),
            pltpu.VMEM((2, DEPTH, 2) + tile, f32),
            pltpu.VMEM((2, DEPTH, 2) + tile, f32),
            pltpu.VMEM((DEPTH, 2) + tile, f32),
            pltpu.VMEM((2, DEPTH, 2) + tile, f32),
            pltpu.VMEM((DEPTH, 2, ENERGIES) + tile, f32),
            pltpu.VMEM((DEPTH, 2, TERMS) + tile, f32),
            pltpu.VMEM((2 * ROWS, LANES), f32),
            pltpu.VMEM((2, n_y, ROWS, LANES), f32),
            pltpu.VMEM((2, 2, 2 * ROWS, LANES), f32),
            pltpu.SemaphoreType.DMA((6,)),
            pltpu.SemaphoreType.DMA((6,)),
            pltpu.SemaphoreType.DMA((6,)),
            pltpu.SemaphoreType.DMA((2, 3)),
            pltpu.SemaphoreType.DMA((2, 3)),
            pltpu.SemaphoreType.DMA((4, n_y)),
            pltpu.SemaphoreType.DMA((4, n_y)),
        ],
        compiler_params=pltpu.CompilerParams(
            collective_id=0, has_side_effects=True, vmem_limit_bytes=56 * 1024 * 1024
        ),
    )(scal, coefficients, checkpoints, adjoints_in, vector_bits, potential_int, residual)
    return gradient, adjoint_out


def solution(mesh):
    fits = mesh.shape["row"] == 2 and mesh.shape["col"] > 2 and mesh.shape["vec"] == 4
    return jax.shard_map(
        windowed if fits else per_device,
        mesh=mesh,
        in_specs=(
            P(None, None, "vec", "row", "col"),
            P(None, "vec", "row", "col"),
            P("vec", "row", "col"),
            P("row", "col"),
            P(),
            P(),
            P(None, "row", "col"),
            P(),
        ),
        out_specs=(P("row", "col"), P(None, "vec", "row", "col")),
        check_vma=False,
    )
```

```python
import math

import jax
import jax.numpy as jnp
from jax import lax
from jax.experimental import pallas as pl
from jax.experimental.pallas import tpu as pltpu
from jax.sharding import PartitionSpec as P

SEG = 16
MOMENTS = 1024
QMAX = 32767


def extended_2(value, sides, width):
    for axis, dim in sides:
        devices, length = (lax.axis_size(axis), value.shape[dim])
        up = [(i, (i + 1) % devices) for i in range(devices)]
        down = [(j, i) for i, j in up]
        last = lax.slice_in_dim(value, length - width, length, axis=dim)
        initial = lax.slice_in_dim(value, 0, width, axis=dim)
        before = lax.ppermute(last, axis, up)
        after = lax.ppermute(initial, axis, down)
        value = jnp.concatenate([before, value, after], axis=dim)
    return value


def window_coefs(first_segment, energies):
    moment_order = first_segment[0] * SEG + jnp.arange(2 * SEG, dtype=jnp.int32)
    degree = moment_order.astype(jnp.float32)
    kernel_norm = float(MOMENTS + 1)
    angle_step = math.pi / kernel_norm
    jackson = (
        (kernel_norm - degree) * jnp.cos(angle_step * degree)
        + jnp.sin(angle_step * degree) * (math.cos(angle_step) / math.sin(angle_step))
    ) / kernel_norm
    factor = jnp.where(moment_order == 0, 1.0, 2.0).astype(jnp.float32)
    angles = jnp.arccos(energies)
    cosines = jnp.cos(degree[:, None] * angles[None, :])
    return (jackson * factor)[:, None] * cosines / (math.pi * jnp.sin(angles))[None, :]


def stencil(extended, onsite, inv_span):
    middle = extended[..., 1:-1, 1:-1]
    beside = (
        extended[..., 2:, 1:-1]
        + extended[..., :-2, 1:-1]
        + extended[..., 1:-1, 2:]
        + extended[..., 1:-1, :-2]
    )
    return inv_span * (onsite * middle - beside)


def per_device(
    checkpoints,
    adjoints_in,
    vector_bits,
    potential_int,
    pot_scale,
    energies,
    residual,
    first_segment,
):
    pot_factor = pot_scale[0]
    inv_span = 1.0 / (4.5 + QMAX * pot_factor)
    onsite = potential_int.astype(jnp.float32) * pot_factor
    coefficients = window_coefs(first_segment, energies)
    vector_count = lax.axis_size("vec") * vector_bits.shape[0]
    inv_count = 1.0 / vector_count
    sign_weights = (2 * vector_bits - 1).astype(jnp.float32) * inv_count
    earlier = checkpoints[:, 0]
    current = checkpoints[:, 1]
    zero_grad = jnp.zeros(onsite.shape, jnp.float32)
    carried = (adjoints_in[0], adjoints_in[1], zero_grad)
    weights = jnp.einsum("ne,eij->nij", coefficients, residual, precision=lax.Precision.HIGHEST)

    def forward_step(pair_state, unused):
        before, now = pair_state
        padded = extended_2(now, (("row", 2), ("col", 3)), 1)
        advanced = 2.0 * stencil(padded, onsite, inv_span) - before
        return ((now, advanced), advanced)

    _, generated = lax.scan(forward_step, (earlier, current), None, length=SEG - 2)
    states = jnp.concatenate([earlier[None], current[None], generated], axis=0)

    def adjoint_step(step_carry, inputs):
        after_one, after_two, accum_grad = step_carry
        state_now, weight_now = inputs
        padded = extended_2(after_one, (("row", 1), ("col", 2)), 1)
        accum_grad = accum_grad + jnp.sum(after_one * state_now, axis=0)
        advanced = weight_now * sign_weights + 2.0 * stencil(padded, onsite, inv_span) - after_two
        return ((advanced, after_one, accum_grad), None)

    for segment in (1, 0):
        carried, _ = lax.scan(
            adjoint_step,
            carried,
            (states[:, segment], weights[segment * SEG : (segment + 1) * SEG]),
            reverse=True,
        )
    adjoint_zero, adjoint_first, accum_grad = carried
    gradient = lax.psum(accum_grad, "vec") * (2.0 * inv_span)
    return (gradient, jnp.stack([adjoint_zero, adjoint_first]))


MESH = pl.DeviceIdType.MESH
TERMS = 2 * SEG
ROWS = 32
LANES = 128
REACH = 32
DEPTH = 8
ENERGIES = 16
X_CK, X_ADJ, X_BITS, X_POT, X_RES, X_OUT, H_CK, H_ADJ, H_BITS = range(9)
Z_CK, Z_ADJ, Z_RES = range(3)
V_ROWS, V_HALO, V_GRAD, V_CROSS = range(4)
QUARTER = 4


def pick(lane, parts):
    width = LANES // len(parts)
    while len(parts) > 1:
        parts = [jnp.where((lane & width) == 0, low, high) for low, high in zip(parts[::2], parts[1::2])]
        width = 2 * width
    return parts[0]


def turn(value, shift):
    shift = shift % LANES
    return value if shift == 0 else pltpu.roll(value, shift, 1)


def kernel(
    scal, coefs, ck, adj, bits, pot, res, grad_out, adj_out,
    hck, hadj, hbits, wck, wadj, wbits, wpot, wres, zsend, zrecv, zres, states, even, odd, adj_even, adj_odd, onsite, signs, rwin, weights,
    gbuf, gall, obuf, ls, xs, xr, zs, zr, vs, vr,
):
    x = lax.axis_index("row")
    z = lax.axis_index("col")
    y = lax.axis_index("vec")
    n_z = lax.axis_size("col")
    n_y = lax.axis_size("vec")
    across = {"row": 1 - x}
    right = {"col": lax.rem(z + 1, n_z)}
    left = {"col": lax.rem(z + n_z - 1, n_z)}
    corners = [{"row": 1 - x, **right}, {"row": 1 - x, **left}]
    peers = [{"vec": lax.rem(y + d, n_y)} for d in range(1, n_y)]
    far = [{"row": 1 - x, "vec": lax.rem(y + d, n_y)} for d in range(n_y)]

    own = pl.ds(0, ROWS)
    other = pl.ds(ROWS, ROWS)
    theirs = pl.ds(2 * (1 - x), 2)
    mine = pl.ds(2 * x, 2)

    def local(source, target, index):
        copy = pltpu.make_async_copy(source, target, ls.at[index])
        copy.start()
        return copy

    l_res = local(res, wres.at[:, own], X_RES)
    l_ck = local(ck.at[:, :, mine], wck.at[:, :, :, own], X_CK)
    l_adj = local(adj.at[:, mine], wadj.at[:, :, own], X_ADJ)
    l_bits = local(bits.at[mine], wbits.at[:, own], X_BITS)
    l_pot = local(pot, wpot.at[own], X_POT)
    h_ck = local(ck, hck, H_CK)
    h_adj = local(adj, hadj, H_ADJ)
    h_bits = local(bits, hbits, H_BITS)

    barrier = pltpu.get_barrier_semaphore()
    for device in [right, left] + corners + peers + far:
        pl.semaphore_signal(barrier, inc=1, device_id=device, device_id_type=MESH)
    pl.semaphore_wait(barrier, 4 + len(peers) + len(far))

    def remote(source, target, send, recv, device):
        copy = pltpu.make_async_remote_copy(
            src_ref=source, dst_ref=target, send_sem=send, recv_sem=recv,
            device_id=device, device_id_type=MESH,
        )
        copy.start()
        return copy

    def to_x(source, target, index):
        return remote(source, target, xs.at[index], xr.at[index], across)

    share = pl.ds(QUARTER * y, QUARTER)
    c_res = to_x(res.at[share], wres.at[share, other], X_RES)
    c_ck = to_x(ck.at[:, :, theirs], wck.at[:, :, :, other], X_CK)

    lane = lax.broadcasted_iota(jnp.int32, (8, LANES), 1)

    def rows(j):
        return pl.ds(j, 8, stride=8)

    def pack(slot, side, planes):
        width = LANES // len(planes)
        for i in range(ROWS // 8):
            span = pl.ds(8 * i, 8)
            parts = [plane(span) for plane in planes]
            zsend[side, 0, slot, span] = pick(lane, [turn(w, width * (q + 1)) for q, w in enumerate(parts)])
            zsend[side, 1, slot, span] = pick(lane, [turn(w, width * q) for q, w in enumerate(parts)])

    def unpack(pair, q, count):
        width = LANES // count
        from_left = turn(pair[0], LANES - width - width * q)
        from_right = turn(pair[1], LANES - width * q)
        return jnp.where(lane < LANES // 2, from_right, from_left)

    def to_z(part, slots, target, both=True):
        copies = []
        for side, devices, place in ((0, (right, left), own), (1, corners, other)):
            for d, device in enumerate(devices):
                sems = (zs.at[side, d, part], zr.at[side, d, part])
                copies.append(remote(zsend.at[side if both else 0, d, slots], target(d, place), *sems, device))
        return copies

    def fan(part, source, target, devices):
        return [
            remote(source, target, vs.at[part, d], vr.at[part, d], device) for d, device in enumerate(devices)
        ]

    def to_peers(part, ref):
        return fan(part, ref, ref, peers)

    def settle(copies):
        for copy in copies:
            copy.wait()

    pot_factor = scal[0]
    twice = scal[1]
    inv_count = scal[2]

    l_res.wait()
    pack(3, 0, [lambda span, q=q: wres[QUARTER * y + q, span] for q in range(QUARTER)])
    z_res = to_z(Z_RES, 3, lambda d, place: zres.at[d, y, place], False)
    h_ck.wait()
    for side, first in ((0, 2 * x), (1, 2 * (1 - x))):
        order = [(s, k, v) for s in range(2) for k in range(2) for v in range(2)]
        pack(0, side, [lambda span, s=s, k=k, v=v: hck[s, k, first + v, span] for s, k, v in order])
    z_ck = to_z(Z_CK, pl.ds(0, 1), lambda d, place: zrecv.at[d, pl.ds(0, 1), place])

    c_adj = to_x(adj.at[:, theirs], wadj.at[:, :, other], X_ADJ)
    c_bits = to_x(bits.at[theirs], wbits.at[:, other], X_BITS)
    c_pot = to_x(pot, wpot.at[other], X_POT)
    settle([h_adj, h_bits, l_pot])

    def sign_of(bit):
        return (2 * bit - 1).astype(jnp.float32) * inv_count

    def site_of(level):
        return level.astype(jnp.float32) * pot_factor * twice

    for side, first in ((0, 2 * x), (1, 2 * (1 - x))):
        order = [(k, v) for k in range(2) for v in range(2)]
        pack(1, side, [lambda span, k=k, v=v: hadj[k, first + v, span] for k, v in order])
        marks = [lambda span, v=v: sign_of(hbits[first + v, span]) for v in range(2)]
        pack(2, side, marks + [lambda span: site_of(wpot[span])] * 2)
    z_adj = to_z(Z_ADJ, pl.ds(1, 2), lambda d, place: zrecv.at[d, pl.ds(1, 2), place])

    c_res.wait()
    g_rows = to_peers(V_ROWS, wres.at[share, other])
    settle(z_res)
    g_halo = to_peers(V_HALO, zres.at[:, y])

    l_ck.wait()
    c_ck.wait()
    for j in range(DEPTH):
        planes = [wck[s, k, v, rows(j)] for s in range(2) for k in range(2) for v in range(2)]
        for q, plane in enumerate(planes):
            s, k, v = q // 4, q // 2 % 2, q % 2
            states[s * SEG + k, v, j] = plane
            (even, odd)[k][s, v, j, 0] = plane
    settle(z_ck)
    for j in range(DEPTH):
        pair = [zrecv[d, 0, rows(j)] for d in range(2)]
        for q in range(8):
            s, k, v = q // 4, q // 2 % 2, q % 2
            (even, odd)[k][s, v, j, 1] = unpack(pair, q, 8)

    settle([l_adj, l_bits, c_adj, c_bits, c_pot])
    for j in range(DEPTH):
        planes = [wadj[k, v, rows(j)] for k in range(2) for v in range(2)]
        for q, plane in enumerate(planes):
            (adj_even, adj_odd)[q // 2][q % 2, j, 0] = plane
        signs[0, j, 0] = sign_of(wbits[0, rows(j)])
        signs[1, j, 0] = sign_of(wbits[1, rows(j)])
        onsite[j, 0] = site_of(wpot[rows(j)])

    def halves(value):
        high = value.astype(jnp.bfloat16)
        return high, (value - high.astype(jnp.float32)).astype(jnp.bfloat16)

    def spread(value):
        pick_t = lax.broadcasted_iota(jnp.int32, (TERMS * 8, TERMS), 0) >> 3
        pick_t = pick_t == lax.broadcasted_iota(jnp.int32, (TERMS * 8, TERMS), 1)
        pick_e = lax.broadcasted_iota(jnp.int32, (ENERGIES, ENERGIES * 8), 1) >> 3
        pick_e = pick_e == lax.broadcasted_iota(jnp.int32, (ENERGIES, ENERGIES * 8), 0)
        same = lax.broadcasted_iota(jnp.int32, (TERMS * 8, ENERGIES * 8), 0)
        same = (same & 7) == (lax.broadcasted_iota(jnp.int32, (TERMS * 8, ENERGIES * 8), 1) & 7)
        flag = lambda mask: jnp.where(mask, 1.0, 0.0).astype(jnp.bfloat16)
        tall = jnp.dot(flag(pick_t), value, preferred_element_type=jnp.float32).astype(jnp.bfloat16)
        wide = jnp.dot(tall, flag(pick_e), preferred_element_type=jnp.float32)
        return jnp.where(same, wide, 0.0).astype(jnp.bfloat16)

    kron_high, kron_low = [spread(part) for part in halves(coefs[...])]

    kron_wide = jnp.concatenate([kron_high, kron_high], axis=1)

    def weigh(c):
        for j in range(0, DEPTH, 2):
            block = [rwin[j + i, c].reshape(ENERGIES * 8, LANES) for i in range(2)]
            high, low = halves(jnp.concatenate(block, axis=1))
            total = jnp.dot(kron_wide, jnp.concatenate([high, low], axis=0), preferred_element_type=jnp.float32)
            total = total + jnp.dot(kron_low, high, preferred_element_type=jnp.float32)
            for i in range(2):
                weights[j + i, c] = total[:, i * LANES : (i + 1) * LANES].reshape(TERMS, 8, LANES)

    settle(g_rows)
    for j in range(DEPTH):
        for e in range(ENERGIES):
            rwin[j, 0, e] = wres[e, rows(j)]
    weigh(0)

    settle(z_adj)
    for j in range(DEPTH):
        pair = [zrecv[d, 1, rows(j)] for d in range(2)]
        for q in range(4):
            (adj_even, adj_odd)[q // 2][q % 2, j, 1] = unpack(pair, q, 4)
        pair = [zrecv[d, 2, rows(j)] for d in range(2)]
        signs[0, j, 1] = unpack(pair, 0, 4)
        signs[1, j, 1] = unpack(pair, 1, 4)
        onsite[j, 1] = unpack(pair, 2, 4)

    first_lane = lane == 0
    last_lane = lane == LANES - 1

    def beside(ref, v, j):
        here = [ref[v, j, c] for c in range(2)]
        back = [pltpu.roll(w, 1, 1) for w in here]
        ahead = [pltpu.roll(w, LANES - 1, 1) for w in here]
        sums = []
        for c in range(2):
            before = jnp.where(first_lane, back[1 - c], back[c])
            after = jnp.where(last_lane, ahead[1 - c], ahead[c])
            if j == 0:
                above = pltpu.roll(ref[v, DEPTH - 1, c], 1, 0)
            else:
                above = ref[v, j - 1, c]
            if j == DEPTH - 1:
                below = pltpu.roll(ref[v, 0, c], 7, 0)
            else:
                below = ref[v, j + 1, c]
            sums.append((above + below) + (before + after))
        return here, sums

    def forward(half, carry):
        for step in range(2):
            now, then = (odd, even) if step == 0 else (even, odd)
            k = 2 + 2 * half + step
            for s in range(2):
                for v in range(2):
                    for j in range(DEPTH):
                        here, sums = beside(now.at[s], v, j)
                        for c in range(2):
                            value = (onsite[j, c] * here[c] - twice * sums[c]) - then[s, v, j, c]
                            then[s, v, j, c] = value
                            if c == 0:
                                states[s * SEG + k, v, j] = value
        return carry

    lax.fori_loop(0, SEG // 2 - 1, forward, 0)

    settle(g_halo)
    for j in range(DEPTH):
        for e in range(ENERGIES):
            pair = [zres[d, e // QUARTER, rows(j)] for d in range(2)]
            rwin[j, 1, e] = unpack(pair, e % QUARTER, QUARTER)
    weigh(1)

    def adjoint(half, sums_in):
        grads = list(sums_in)
        for step in range(2):
            now, then = (adj_even, adj_odd) if step == 0 else (adj_odd, adj_even)
            t = TERMS - 1 - step - 2 * half
            for v in range(2):
                for j in range(DEPTH):
                    here, sums = beside(now, v, j)
                    grads[j] = grads[j] + here[0] * states[t, v, j]
                    for c in range(2):
                        source = weights[j, c, t] * signs[v, j, c]
                        then[v, j, c] = (source + onsite[j, c] * here[c]) - (twice * sums[c] + then[v, j, c])
        return tuple(grads)

    zero = jnp.zeros((8, LANES), jnp.float32)
    grads = lax.fori_loop(0, TERMS // 2, adjoint, (zero,) * DEPTH)

    for j in range(DEPTH):
        gbuf[rows(j)] = grads[j]
        for k in range(2):
            for v in range(2):
                obuf[k, v, rows(j)] = (adj_even, adj_odd)[k][v, j, 0]
    sums = fan(V_CROSS, gbuf.at[other], gall.at[x, y], far)
    gall[x, y] = gbuf[own]
    sums += to_peers(V_GRAD, gall.at[x, y])
    c_out = to_x(obuf.at[:, :, other], adj_out.at[:, mine], X_OUT)
    l_out = local(obuf.at[:, :, own], adj_out.at[:, mine], X_OUT)
    settle(sums)
    total = gall[0, 0] + gall[1, 0]
    for d in range(1, n_y):
        total = total + (gall[0, d] + gall[1, d])
    gbuf[own] = total * twice
    l_grad = local(gbuf.at[own], grad_out, X_CK)
    l_out.wait()
    c_out.wait()
    l_grad.wait()


def windowed(
    checkpoints,
    adjoints_in,
    vector_bits,
    potential_int,
    pot_scale,
    energies,
    residual,
    first_segment,
):
    n_y = lax.axis_size("vec")
    pot_factor = pot_scale[0]
    twice = 2.0 / (4.5 + QMAX * pot_factor)
    coefficients = window_coefs(first_segment, energies)
    inv_count = 1.0 / (n_y * vector_bits.shape[0])
    scal = jnp.stack([pot_factor, twice, jnp.float32(inv_count)])
    f32, i32 = jnp.float32, jnp.int32
    vmem = pl.BlockSpec(memory_space=pltpu.VMEM)
    tile = (8, LANES)
    gradient, adjoint_out = pl.pallas_call(
        kernel,
        out_shape=(
            jax.ShapeDtypeStruct(potential_int.shape, f32),
            jax.ShapeDtypeStruct(adjoints_in.shape, f32),
        ),
        in_specs=[pl.BlockSpec(memory_space=pltpu.SMEM), vmem] + [pl.BlockSpec(memory_space=pl.ANY)] * 5,
        out_specs=(pl.BlockSpec(memory_space=pl.ANY),) * 2,
        scratch_shapes=[
            pltpu.VMEM(checkpoints.shape, f32),
            pltpu.VMEM(adjoints_in.shape, f32),
            pltpu.VMEM(vector_bits.shape, i32),
            pltpu.VMEM((2, 2, 2, 2 * ROWS, LANES), f32),
            pltpu.VMEM((2, 2, 2 * ROWS, LANES), f32),
            pltpu.VMEM((2, 2 * ROWS, LANES), i32),
            pltpu.VMEM((2 * ROWS, LANES), i32),
            pltpu.VMEM((ENERGIES, 2 * ROWS, LANES), f32),
            pltpu.VMEM((2, 2, 4, ROWS, LANES), f32),
            pltpu.VMEM((2, 3, 2 * ROWS, LANES), f32),
            pltpu.VMEM((2, n_y, 2 * ROWS, LANES), f32),
            pltpu.VMEM((TERMS, 2, DEPTH) + tile, f32),
            pltpu.VMEM((2, 2, DEPTH, 2) + tile, f32),
            pltpu.VMEM((2, 2, DEPTH, 2) + tile, f32),
            pltpu.VMEM((2, DEPTH, 2) + tile, f32),
            pltpu.VMEM((2, DEPTH, 2) + tile, f32),
            pltpu.VMEM((DEPTH, 2) + tile, f32),
            pltpu.VMEM((2, DEPTH, 2) + tile, f32),
            pltpu.VMEM((DEPTH, 2, ENERGIES) + tile, f32),
            pltpu.VMEM((DEPTH, 2, TERMS) + tile, f32),
            pltpu.VMEM((2 * ROWS, LANES), f32),
            pltpu.VMEM((2, n_y, ROWS, LANES), f32),
            pltpu.VMEM((2, 2, 2 * ROWS, LANES), f32),
            pltpu.SemaphoreType.DMA((9,)),
            pltpu.SemaphoreType.DMA((6,)),
            pltpu.SemaphoreType.DMA((6,)),
            pltpu.SemaphoreType.DMA((2, 2, 3)),
            pltpu.SemaphoreType.DMA((2, 2, 3)),
            pltpu.SemaphoreType.DMA((4, n_y)),
            pltpu.SemaphoreType.DMA((4, n_y)),
        ],
        compiler_params=pltpu.CompilerParams(
            collective_id=0, has_side_effects=True, vmem_limit_bytes=56 * 1024 * 1024
        ),
    )(scal, coefficients, checkpoints, adjoints_in, vector_bits, potential_int, residual)
    return gradient, adjoint_out


def solution(mesh):
    fits = mesh.shape["row"] == 2 and mesh.shape["col"] > 2 and mesh.shape["vec"] == 4
    return jax.shard_map(
        windowed if fits else per_device,
        mesh=mesh,
        in_specs=(
            P(None, None, "vec", "row", "col"),
            P(None, "vec", "row", "col"),
            P("vec", "row", "col"),
            P("row", "col"),
            P(),
            P(),
            P(None, "row", "col"),
            P(),
        ),
        out_specs=(P("row", "col"), P(None, "vec", "row", "col")),
        check_vma=False,
    )
```

```python
import math

import jax
import jax.numpy as jnp
from jax import lax
from jax.experimental import pallas as pl
from jax.experimental.pallas import tpu as pltpu
from jax.sharding import PartitionSpec as P

SEG = 16
MOMENTS = 1024
QMAX = 32767


def extended_2(value, sides, width):
    for axis, dim in sides:
        devices, length = (lax.axis_size(axis), value.shape[dim])
        up = [(i, (i + 1) % devices) for i in range(devices)]
        down = [(j, i) for i, j in up]
        last = lax.slice_in_dim(value, length - width, length, axis=dim)
        initial = lax.slice_in_dim(value, 0, width, axis=dim)
        before = lax.ppermute(last, axis, up)
        after = lax.ppermute(initial, axis, down)
        value = jnp.concatenate([before, value, after], axis=dim)
    return value


def window_coefs(first_segment, energies):
    moment_order = first_segment[0] * SEG + jnp.arange(2 * SEG, dtype=jnp.int32)
    degree = moment_order.astype(jnp.float32)
    kernel_norm = float(MOMENTS + 1)
    angle_step = math.pi / kernel_norm
    jackson = (
        (kernel_norm - degree) * jnp.cos(angle_step * degree)
        + jnp.sin(angle_step * degree) * (math.cos(angle_step) / math.sin(angle_step))
    ) / kernel_norm
    factor = jnp.where(moment_order == 0, 1.0, 2.0).astype(jnp.float32)
    angles = jnp.arccos(energies)
    cosines = jnp.cos(degree[:, None] * angles[None, :])
    return (jackson * factor)[:, None] * cosines / (math.pi * jnp.sin(angles))[None, :]


def stencil(extended, onsite, inv_span):
    middle = extended[..., 1:-1, 1:-1]
    beside = (
        extended[..., 2:, 1:-1]
        + extended[..., :-2, 1:-1]
        + extended[..., 1:-1, 2:]
        + extended[..., 1:-1, :-2]
    )
    return inv_span * (onsite * middle - beside)


def per_device(
    checkpoints,
    adjoints_in,
    vector_bits,
    potential_int,
    pot_scale,
    energies,
    residual,
    first_segment,
):
    pot_factor = pot_scale[0]
    inv_span = 1.0 / (4.5 + QMAX * pot_factor)
    onsite = potential_int.astype(jnp.float32) * pot_factor
    coefficients = window_coefs(first_segment, energies)
    vector_count = lax.axis_size("vec") * vector_bits.shape[0]
    inv_count = 1.0 / vector_count
    sign_weights = (2 * vector_bits - 1).astype(jnp.float32) * inv_count
    earlier = checkpoints[:, 0]
    current = checkpoints[:, 1]
    zero_grad = jnp.zeros(onsite.shape, jnp.float32)
    carried = (adjoints_in[0], adjoints_in[1], zero_grad)
    weights = jnp.einsum("ne,eij->nij", coefficients, residual, precision=lax.Precision.HIGHEST)

    def forward_step(pair_state, unused):
        before, now = pair_state
        padded = extended_2(now, (("row", 2), ("col", 3)), 1)
        advanced = 2.0 * stencil(padded, onsite, inv_span) - before
        return ((now, advanced), advanced)

    _, generated = lax.scan(forward_step, (earlier, current), None, length=SEG - 2)
    states = jnp.concatenate([earlier[None], current[None], generated], axis=0)

    def adjoint_step(step_carry, inputs):
        after_one, after_two, accum_grad = step_carry
        state_now, weight_now = inputs
        padded = extended_2(after_one, (("row", 1), ("col", 2)), 1)
        accum_grad = accum_grad + jnp.sum(after_one * state_now, axis=0)
        advanced = weight_now * sign_weights + 2.0 * stencil(padded, onsite, inv_span) - after_two
        return ((advanced, after_one, accum_grad), None)

    for segment in (1, 0):
        carried, _ = lax.scan(
            adjoint_step,
            carried,
            (states[:, segment], weights[segment * SEG : (segment + 1) * SEG]),
            reverse=True,
        )
    adjoint_zero, adjoint_first, accum_grad = carried
    gradient = lax.psum(accum_grad, "vec") * (2.0 * inv_span)
    return (gradient, jnp.stack([adjoint_zero, adjoint_first]))


MESH = pl.DeviceIdType.MESH
TERMS = 2 * SEG
ROWS = 32
LANES = 128
REACH = 32
DEPTH = 8
ENERGIES = 16
X_CK, X_ADJ, X_BITS, X_POT, X_RES, X_OUT, H_CK, H_ADJ, H_BITS = range(9)
Z_CK, Z_ADJ, Z_RES = range(3)
V_ROWS, V_HALO, V_GRAD, V_CROSS = range(4)
QUARTER = 4


def pick(lane, parts):
    width = LANES // len(parts)
    while len(parts) > 1:
        parts = [jnp.where((lane & width) == 0, low, high) for low, high in zip(parts[::2], parts[1::2])]
        width = 2 * width
    return parts[0]


def turn(value, shift):
    shift = shift % LANES
    return value if shift == 0 else pltpu.roll(value, shift, 1)


def kernel(
    scal, coefs, ck, adj, bits, pot, res, grad_out, adj_out,
    hck, hadj, hbits, wck, wadj, wbits, wpot, wres, zsend, zrecv, zres, states, even, odd, adj_even, adj_odd, onsite, signs, rwin, weights,
    gbuf, gall, obuf, ls, xs, xr, zs, zr, vs, vr,
):
    x = lax.axis_index("row")
    z = lax.axis_index("col")
    y = lax.axis_index("vec")
    n_z = lax.axis_size("col")
    n_y = lax.axis_size("vec")
    across = {"row": 1 - x}
    right = {"col": lax.rem(z + 1, n_z)}
    left = {"col": lax.rem(z + n_z - 1, n_z)}
    corners = [{"row": 1 - x, **right}, {"row": 1 - x, **left}]
    peers = [{"vec": lax.rem(y + d, n_y)} for d in range(1, n_y)]
    far = [{"row": 1 - x, "vec": lax.rem(y + d, n_y)} for d in range(n_y)]

    own = pl.ds(0, ROWS)
    other = pl.ds(ROWS, ROWS)
    theirs = pl.ds(2 * (1 - x), 2)
    mine = pl.ds(2 * x, 2)

    def local(source, target, index):
        copy = pltpu.make_async_copy(source, target, ls.at[index])
        copy.start()
        return copy

    l_res = local(res, wres.at[:, own], X_RES)
    l_ck = local(ck.at[:, :, mine], wck.at[:, :, :, own], X_CK)
    l_adj = local(adj.at[:, mine], wadj.at[:, :, own], X_ADJ)
    l_bits = local(bits.at[mine], wbits.at[:, own], X_BITS)
    l_pot = local(pot, wpot.at[own], X_POT)
    h_ck = local(ck, hck, H_CK)
    h_adj = local(adj, hadj, H_ADJ)
    h_bits = local(bits, hbits, H_BITS)

    barrier = pltpu.get_barrier_semaphore()
    for device in [right, left] + corners + peers + far:
        pl.semaphore_signal(barrier, inc=1, device_id=device, device_id_type=MESH)
    pl.semaphore_wait(barrier, 4 + len(peers) + len(far))

    def remote(source, target, send, recv, device):
        copy = pltpu.make_async_remote_copy(
            src_ref=source, dst_ref=target, send_sem=send, recv_sem=recv,
            device_id=device, device_id_type=MESH,
        )
        copy.start()
        return copy

    def to_x(source, target, index):
        return remote(source, target, xs.at[index], xr.at[index], across)

    share = pl.ds(QUARTER * y, QUARTER)
    c_res = to_x(res.at[share], wres.at[share, other], X_RES)
    c_ck = to_x(ck.at[:, :, theirs], wck.at[:, :, :, other], X_CK)

    lane = lax.broadcasted_iota(jnp.int32, (8, LANES), 1)

    def rows(j):
        return pl.ds(j, 8, stride=8)

    def pack(slot, side, planes):
        width = LANES // len(planes)
        for i in range(ROWS // 8):
            span = pl.ds(8 * i, 8)
            parts = [plane(span) for plane in planes]
            zsend[side, 0, slot, span] = pick(lane, [turn(w, width * (q + 1)) for q, w in enumerate(parts)])
            zsend[side, 1, slot, span] = pick(lane, [turn(w, width * q) for q, w in enumerate(parts)])

    def unpack(pair, q, count):
        width = LANES // count
        from_left = turn(pair[0], LANES - width - width * q)
        from_right = turn(pair[1], LANES - width * q)
        return jnp.where(lane < LANES // 2, from_right, from_left)

    def to_z(part, slots, target, both=True):
        copies = []
        for side, devices, place in ((0, (right, left), own), (1, corners, other)):
            for d, device in enumerate(devices):
                sems = (zs.at[side, d, part], zr.at[side, d, part])
                copies.append(remote(zsend.at[side if both else 0, d, slots], target(d, place), *sems, device))
        return copies

    def fan(part, source, target, devices):
        return [
            remote(source, target, vs.at[part, d], vr.at[part, d], device) for d, device in enumerate(devices)
        ]

    def to_peers(part, ref):
        return fan(part, ref, ref, peers)

    def settle(copies):
        for copy in copies:
            copy.wait()

    pot_factor = scal[0]
    twice = scal[1]
    inv_count = scal[2]

    l_res.wait()
    pack(3, 0, [lambda span, q=q: wres[QUARTER * y + q, span] for q in range(QUARTER)])
    z_res = to_z(Z_RES, 3, lambda d, place: zres.at[d, y, place], False)
    h_ck.wait()
    for side, first in ((0, 2 * x), (1, 2 * (1 - x))):
        order = [(s, k, v) for s in range(2) for k in range(2) for v in range(2)]
        pack(0, side, [lambda span, s=s, k=k, v=v: hck[s, k, first + v, span] for s, k, v in order])
    z_ck = to_z(Z_CK, pl.ds(0, 1), lambda d, place: zrecv.at[d, pl.ds(0, 1), place])

    c_adj = to_x(adj.at[:, theirs], wadj.at[:, :, other], X_ADJ)
    c_bits = to_x(bits.at[theirs], wbits.at[:, other], X_BITS)
    c_pot = to_x(pot, wpot.at[other], X_POT)
    settle([h_adj, h_bits, l_pot])

    def sign_of(bit):
        return (2 * bit - 1).astype(jnp.float32) * inv_count

    def site_of(level):
        return level.astype(jnp.float32) * pot_factor * twice

    for side, first in ((0, 2 * x), (1, 2 * (1 - x))):
        order = [(k, v) for k in range(2) for v in range(2)]
        pack(1, side, [lambda span, k=k, v=v: hadj[k, first + v, span] for k, v in order])
        marks = [lambda span, v=v: sign_of(hbits[first + v, span]) for v in range(2)]
        pack(2, side, marks + [lambda span: site_of(wpot[span])] * 2)
    z_adj = to_z(Z_ADJ, pl.ds(1, 2), lambda d, place: zrecv.at[d, pl.ds(1, 2), place])

    c_res.wait()
    g_rows = to_peers(V_ROWS, wres.at[share, other])
    settle(z_res)
    g_halo = to_peers(V_HALO, zres.at[:, y])

    l_ck.wait()
    c_ck.wait()
    for j in range(DEPTH):
        planes = [wck[s, k, v, rows(j)] for s in range(2) for k in range(2) for v in range(2)]
        for q, plane in enumerate(planes):
            s, k, v = q // 4, q // 2 % 2, q % 2
            states[s * SEG + k, v, j] = plane
            (even, odd)[k][s, v, j, 0] = plane
    settle(z_ck)
    for j in range(DEPTH):
        pair = [zrecv[d, 0, rows(j)] for d in range(2)]
        for q in range(8):
            s, k, v = q // 4, q // 2 % 2, q % 2
            (even, odd)[k][s, v, j, 1] = unpack(pair, q, 8)

    settle([l_adj, l_bits, c_adj, c_bits, c_pot])
    for j in range(DEPTH):
        planes = [wadj[k, v, rows(j)] for k in range(2) for v in range(2)]
        for q, plane in enumerate(planes):
            (adj_even, adj_odd)[q // 2][q % 2, j, 0] = plane
        signs[0, j, 0] = sign_of(wbits[0, rows(j)])
        signs[1, j, 0] = sign_of(wbits[1, rows(j)])
        onsite[j, 0] = site_of(wpot[rows(j)])

    def halves(value):
        high = value.astype(jnp.bfloat16)
        return high, (value - high.astype(jnp.float32)).astype(jnp.bfloat16)

    def spread(value):
        pick_t = lax.broadcasted_iota(jnp.int32, (TERMS * 8, TERMS), 0) >> 3
        pick_t = pick_t == lax.broadcasted_iota(jnp.int32, (TERMS * 8, TERMS), 1)
        pick_e = lax.broadcasted_iota(jnp.int32, (ENERGIES, ENERGIES * 8), 1) >> 3
        pick_e = pick_e == lax.broadcasted_iota(jnp.int32, (ENERGIES, ENERGIES * 8), 0)
        same = lax.broadcasted_iota(jnp.int32, (TERMS * 8, ENERGIES * 8), 0)
        same = (same & 7) == (lax.broadcasted_iota(jnp.int32, (TERMS * 8, ENERGIES * 8), 1) & 7)
        flag = lambda mask: jnp.where(mask, 1.0, 0.0).astype(jnp.bfloat16)
        tall = jnp.dot(flag(pick_t), value, preferred_element_type=jnp.float32).astype(jnp.bfloat16)
        wide = jnp.dot(tall, flag(pick_e), preferred_element_type=jnp.float32)
        return jnp.where(same, wide, 0.0).astype(jnp.bfloat16)

    kron_high, kron_low = [spread(part) for part in halves(coefs[...])]

    kron_wide = jnp.concatenate([kron_high, kron_high], axis=1)

    def weigh(c):
        for j in range(0, DEPTH, 2):
            block = [rwin[j + i, c].reshape(ENERGIES * 8, LANES) for i in range(2)]
            high, low = halves(jnp.concatenate(block, axis=1))
            total = jnp.dot(kron_wide, jnp.concatenate([high, low], axis=0), preferred_element_type=jnp.float32)
            total = total + jnp.dot(kron_low, high, preferred_element_type=jnp.float32)
            for i in range(2):
                weights[j + i, c] = total[:, i * LANES : (i + 1) * LANES].reshape(TERMS, 8, LANES)

    settle(g_rows)
    for j in range(DEPTH):
        for e in range(ENERGIES):
            rwin[j, 0, e] = wres[e, rows(j)]
    weigh(0)

    settle(z_adj)
    for j in range(DEPTH):
        pair = [zrecv[d, 1, rows(j)] for d in range(2)]
        for q in range(4):
            (adj_even, adj_odd)[q // 2][q % 2, j, 1] = unpack(pair, q, 4)
        pair = [zrecv[d, 2, rows(j)] for d in range(2)]
        signs[0, j, 1] = unpack(pair, 0, 4)
        signs[1, j, 1] = unpack(pair, 1, 4)
        onsite[j, 1] = unpack(pair, 2, 4)

    first_lane = lane == 0
    last_lane = lane == LANES - 1

    def beside(ref, v, j):
        here = [ref[v, j, c] for c in range(2)]
        back = [pltpu.roll(w, 1, 1) for w in here]
        ahead = [pltpu.roll(w, LANES - 1, 1) for w in here]
        sums = []
        for c in range(2):
            before = jnp.where(first_lane, back[1 - c], back[c])
            after = jnp.where(last_lane, ahead[1 - c], ahead[c])
            if j == 0:
                above = pltpu.roll(ref[v, DEPTH - 1, c], 1, 0)
            else:
                above = ref[v, j - 1, c]
            if j == DEPTH - 1:
                below = pltpu.roll(ref[v, 0, c], 7, 0)
            else:
                below = ref[v, j + 1, c]
            sums.append((above + below) + (before + after))
        return here, sums

    def forward(half, carry):
        for step in range(2):
            now, then = (odd, even) if step == 0 else (even, odd)
            k = 2 + 2 * half + step
            for s in range(2):
                for v in range(2):
                    values = []
                    for j in range(DEPTH):
                        here, sums = beside(now.at[s], v, j)
                        for c in range(2):
                            values.append((onsite[j, c] * here[c] - twice * sums[c]) - then[s, v, j, c])
                    for j in range(DEPTH):
                        for c in range(2):
                            then[s, v, j, c] = values[2 * j + c]
                    for j in range(DEPTH):
                        states[s * SEG + k, v, j] = values[2 * j]
        return carry

    lax.fori_loop(0, SEG // 2 - 1, forward, 0)

    settle(g_halo)
    for j in range(DEPTH):
        for e in range(ENERGIES):
            pair = [zres[d, e // QUARTER, rows(j)] for d in range(2)]
            rwin[j, 1, e] = unpack(pair, e % QUARTER, QUARTER)
    weigh(1)

    def adjoint(half, sums_in):
        grads = list(sums_in)
        for step in range(2):
            now, then = (adj_even, adj_odd) if step == 0 else (adj_odd, adj_even)
            t = TERMS - 1 - step - 2 * half
            for v in range(2):
                values = []
                for j in range(DEPTH):
                    here, sums = beside(now, v, j)
                    grads[j] = grads[j] + here[0] * states[t, v, j]
                    for c in range(2):
                        source = weights[j, c, t] * signs[v, j, c]
                        values.append((source + onsite[j, c] * here[c]) - (twice * sums[c] + then[v, j, c]))
                for j in range(DEPTH):
                    for c in range(2):
                        then[v, j, c] = values[2 * j + c]
        return tuple(grads)

    zero = jnp.zeros((8, LANES), jnp.float32)
    grads = lax.fori_loop(0, TERMS // 2, adjoint, (zero,) * DEPTH)

    for j in range(DEPTH):
        gbuf[rows(j)] = grads[j]
        for k in range(2):
            for v in range(2):
                obuf[k, v, rows(j)] = (adj_even, adj_odd)[k][v, j, 0]
    sums = fan(V_CROSS, gbuf.at[other], gall.at[x, y], far)
    gall[x, y] = gbuf[own]
    sums += to_peers(V_GRAD, gall.at[x, y])
    c_out = to_x(obuf.at[:, :, other], adj_out.at[:, mine], X_OUT)
    l_out = local(obuf.at[:, :, own], adj_out.at[:, mine], X_OUT)
    settle(sums)
    total = gall[0, 0] + gall[1, 0]
    for d in range(1, n_y):
        total = total + (gall[0, d] + gall[1, d])
    gbuf[own] = total * twice
    l_grad = local(gbuf.at[own], grad_out, X_CK)
    l_out.wait()
    c_out.wait()
    l_grad.wait()


def windowed(
    checkpoints,
    adjoints_in,
    vector_bits,
    potential_int,
    pot_scale,
    energies,
    residual,
    first_segment,
):
    n_y = lax.axis_size("vec")
    pot_factor = pot_scale[0]
    twice = 2.0 / (4.5 + QMAX * pot_factor)
    coefficients = window_coefs(first_segment, energies)
    inv_count = 1.0 / (n_y * vector_bits.shape[0])
    scal = jnp.stack([pot_factor, twice, jnp.float32(inv_count)])
    f32, i32 = jnp.float32, jnp.int32
    vmem = pl.BlockSpec(memory_space=pltpu.VMEM)
    tile = (8, LANES)
    gradient, adjoint_out = pl.pallas_call(
        kernel,
        out_shape=(
            jax.ShapeDtypeStruct(potential_int.shape, f32),
            jax.ShapeDtypeStruct(adjoints_in.shape, f32),
        ),
        in_specs=[pl.BlockSpec(memory_space=pltpu.SMEM), vmem] + [pl.BlockSpec(memory_space=pl.ANY)] * 5,
        out_specs=(pl.BlockSpec(memory_space=pl.ANY),) * 2,
        scratch_shapes=[
            pltpu.VMEM(checkpoints.shape, f32),
            pltpu.VMEM(adjoints_in.shape, f32),
            pltpu.VMEM(vector_bits.shape, i32),
            pltpu.VMEM((2, 2, 2, 2 * ROWS, LANES), f32),
            pltpu.VMEM((2, 2, 2 * ROWS, LANES), f32),
            pltpu.VMEM((2, 2 * ROWS, LANES), i32),
            pltpu.VMEM((2 * ROWS, LANES), i32),
            pltpu.VMEM((ENERGIES, 2 * ROWS, LANES), f32),
            pltpu.VMEM((2, 2, 4, ROWS, LANES), f32),
            pltpu.VMEM((2, 3, 2 * ROWS, LANES), f32),
            pltpu.VMEM((2, n_y, 2 * ROWS, LANES), f32),
            pltpu.VMEM((TERMS, 2, DEPTH) + tile, f32),
            pltpu.VMEM((2, 2, DEPTH, 2) + tile, f32),
            pltpu.VMEM((2, 2, DEPTH, 2) + tile, f32),
            pltpu.VMEM((2, DEPTH, 2) + tile, f32),
            pltpu.VMEM((2, DEPTH, 2) + tile, f32),
            pltpu.VMEM((DEPTH, 2) + tile, f32),
            pltpu.VMEM((2, DEPTH, 2) + tile, f32),
            pltpu.VMEM((DEPTH, 2, ENERGIES) + tile, f32),
            pltpu.VMEM((DEPTH, 2, TERMS) + tile, f32),
            pltpu.VMEM((2 * ROWS, LANES), f32),
            pltpu.VMEM((2, n_y, ROWS, LANES), f32),
            pltpu.VMEM((2, 2, 2 * ROWS, LANES), f32),
            pltpu.SemaphoreType.DMA((9,)),
            pltpu.SemaphoreType.DMA((6,)),
            pltpu.SemaphoreType.DMA((6,)),
            pltpu.SemaphoreType.DMA((2, 2, 3)),
            pltpu.SemaphoreType.DMA((2, 2, 3)),
            pltpu.SemaphoreType.DMA((4, n_y)),
            pltpu.SemaphoreType.DMA((4, n_y)),
        ],
        compiler_params=pltpu.CompilerParams(
            collective_id=0, has_side_effects=True, vmem_limit_bytes=537 * 1024 * 1024 // 10
        ),
    )(scal, coefficients, checkpoints, adjoints_in, vector_bits, potential_int, residual)
    return gradient, adjoint_out


def solution(mesh):
    fits = mesh.shape["row"] == 2 and mesh.shape["col"] > 2 and mesh.shape["vec"] == 4
    return jax.shard_map(
        windowed if fits else per_device,
        mesh=mesh,
        in_specs=(
            P(None, None, "vec", "row", "col"),
            P(None, "vec", "row", "col"),
            P("vec", "row", "col"),
            P("row", "col"),
            P(),
            P(),
            P(None, "row", "col"),
            P(),
        ),
        out_specs=(P("row", "col"), P(None, "vec", "row", "col")),
        check_vma=False,
    )
```

```python
import math

import jax
import jax.numpy as jnp
from jax import lax
from jax.experimental import pallas as pl
from jax.experimental.pallas import tpu as pltpu
from jax.sharding import PartitionSpec as P

SEG = 16
MOMENTS = 1024
QMAX = 32767


def extended_2(value, sides, width):
    for axis, dim in sides:
        devices, length = (lax.axis_size(axis), value.shape[dim])
        up = [(i, (i + 1) % devices) for i in range(devices)]
        down = [(j, i) for i, j in up]
        last = lax.slice_in_dim(value, length - width, length, axis=dim)
        initial = lax.slice_in_dim(value, 0, width, axis=dim)
        before = lax.ppermute(last, axis, up)
        after = lax.ppermute(initial, axis, down)
        value = jnp.concatenate([before, value, after], axis=dim)
    return value


def window_coefs(first_segment, energies):
    moment_order = first_segment[0] * SEG + jnp.arange(2 * SEG, dtype=jnp.int32)
    degree = moment_order.astype(jnp.float32)
    kernel_norm = float(MOMENTS + 1)
    angle_step = math.pi / kernel_norm
    jackson = (
        (kernel_norm - degree) * jnp.cos(angle_step * degree)
        + jnp.sin(angle_step * degree) * (math.cos(angle_step) / math.sin(angle_step))
    ) / kernel_norm
    factor = jnp.where(moment_order == 0, 1.0, 2.0).astype(jnp.float32)
    angles = jnp.arccos(energies)
    cosines = jnp.cos(degree[:, None] * angles[None, :])
    return (jackson * factor)[:, None] * cosines / (math.pi * jnp.sin(angles))[None, :]


def stencil(extended, onsite, inv_span):
    middle = extended[..., 1:-1, 1:-1]
    beside = (
        extended[..., 2:, 1:-1]
        + extended[..., :-2, 1:-1]
        + extended[..., 1:-1, 2:]
        + extended[..., 1:-1, :-2]
    )
    return inv_span * (onsite * middle - beside)


def per_device(
    checkpoints,
    adjoints_in,
    vector_bits,
    potential_int,
    pot_scale,
    energies,
    residual,
    first_segment,
):
    pot_factor = pot_scale[0]
    inv_span = 1.0 / (4.5 + QMAX * pot_factor)
    onsite = potential_int.astype(jnp.float32) * pot_factor
    coefficients = window_coefs(first_segment, energies)
    vector_count = lax.axis_size("vec") * vector_bits.shape[0]
    inv_count = 1.0 / vector_count
    sign_weights = (2 * vector_bits - 1).astype(jnp.float32) * inv_count
    earlier = checkpoints[:, 0]
    current = checkpoints[:, 1]
    zero_grad = jnp.zeros(onsite.shape, jnp.float32)
    carried = (adjoints_in[0], adjoints_in[1], zero_grad)
    weights = jnp.einsum("ne,eij->nij", coefficients, residual, precision=lax.Precision.HIGHEST)

    def forward_step(pair_state, unused):
        before, now = pair_state
        padded = extended_2(now, (("row", 2), ("col", 3)), 1)
        advanced = 2.0 * stencil(padded, onsite, inv_span) - before
        return ((now, advanced), advanced)

    _, generated = lax.scan(forward_step, (earlier, current), None, length=SEG - 2)
    states = jnp.concatenate([earlier[None], current[None], generated], axis=0)

    def adjoint_step(step_carry, inputs):
        after_one, after_two, accum_grad = step_carry
        state_now, weight_now = inputs
        padded = extended_2(after_one, (("row", 1), ("col", 2)), 1)
        accum_grad = accum_grad + jnp.sum(after_one * state_now, axis=0)
        advanced = weight_now * sign_weights + 2.0 * stencil(padded, onsite, inv_span) - after_two
        return ((advanced, after_one, accum_grad), None)

    for segment in (1, 0):
        carried, _ = lax.scan(
            adjoint_step,
            carried,
            (states[:, segment], weights[segment * SEG : (segment + 1) * SEG]),
            reverse=True,
        )
    adjoint_zero, adjoint_first, accum_grad = carried
    gradient = lax.psum(accum_grad, "vec") * (2.0 * inv_span)
    return (gradient, jnp.stack([adjoint_zero, adjoint_first]))


MESH = pl.DeviceIdType.MESH
TERMS = 2 * SEG
ROWS = 32
LANES = 128
REACH = 32
DEPTH = 8
ENERGIES = 16
X_CK, X_ADJ, X_BITS, X_POT, X_RES, X_OUT, H_CK, H_ADJ, H_BITS = range(9)
Z_CK, Z_ADJ, Z_RES = range(3)
V_ROWS, V_HALO, V_GRAD, V_CROSS = range(4)
QUARTER = 4


def pick(lane, parts):
    width = LANES // len(parts)
    while len(parts) > 1:
        parts = [jnp.where((lane & width) == 0, low, high) for low, high in zip(parts[::2], parts[1::2])]
        width = 2 * width
    return parts[0]


def turn(value, shift):
    shift = shift % LANES
    return value if shift == 0 else pltpu.roll(value, shift, 1)


def kernel(
    scal, coefs, ck, adj, bits, pot, res, grad_out, adj_out,
    hck, hadj, hbits, wck, wadj, wbits, wpot, wres, zsend, zrecv, zres, states, even, odd, adj_even, adj_odd, onsite, signs, rwin, weights,
    gbuf, gall, obuf, ls, xs, xr, zs, zr, vs, vr,
):
    x = lax.axis_index("row")
    z = lax.axis_index("col")
    y = lax.axis_index("vec")
    n_z = lax.axis_size("col")
    n_y = lax.axis_size("vec")
    across = {"row": 1 - x}
    right = {"col": lax.rem(z + 1, n_z)}
    left = {"col": lax.rem(z + n_z - 1, n_z)}
    corners = [{"row": 1 - x, **right}, {"row": 1 - x, **left}]
    peers = [{"vec": lax.rem(y + d, n_y)} for d in range(1, n_y)]
    far = [{"row": 1 - x, "vec": lax.rem(y + d, n_y)} for d in range(n_y)]

    own = pl.ds(0, ROWS)
    other = pl.ds(ROWS, ROWS)
    theirs = pl.ds(2 * (1 - x), 2)
    mine = pl.ds(2 * x, 2)

    def local(source, target, index):
        copy = pltpu.make_async_copy(source, target, ls.at[index])
        copy.start()
        return copy

    l_res = local(res, wres.at[:, own], X_RES)
    l_ck = local(ck.at[:, :, mine], wck.at[:, :, :, own], X_CK)
    l_adj = local(adj.at[:, mine], wadj.at[:, :, own], X_ADJ)
    l_bits = local(bits.at[mine], wbits.at[:, own], X_BITS)
    l_pot = local(pot, wpot.at[own], X_POT)
    h_ck = local(ck, hck, H_CK)
    h_adj = local(adj, hadj, H_ADJ)
    h_bits = local(bits, hbits, H_BITS)

    barrier = pltpu.get_barrier_semaphore()
    for device in [right, left] + corners + peers + far:
        pl.semaphore_signal(barrier, inc=1, device_id=device, device_id_type=MESH)
    pl.semaphore_wait(barrier, 4 + len(peers) + len(far))

    def remote(source, target, send, recv, device):
        copy = pltpu.make_async_remote_copy(
            src_ref=source, dst_ref=target, send_sem=send, recv_sem=recv,
            device_id=device, device_id_type=MESH,
        )
        copy.start()
        return copy

    def to_x(source, target, index):
        return remote(source, target, xs.at[index], xr.at[index], across)

    share = pl.ds(QUARTER * y, QUARTER)
    c_res = to_x(res.at[share], wres.at[share, other], X_RES)
    c_ck = to_x(ck.at[:, :, theirs], wck.at[:, :, :, other], X_CK)

    lane = lax.broadcasted_iota(jnp.int32, (8, LANES), 1)

    def rows(j):
        return pl.ds(j, 8, stride=8)

    def pack(slot, side, planes):
        width = LANES // len(planes)
        for i in range(ROWS // 8):
            span = pl.ds(8 * i, 8)
            parts = [plane(span) for plane in planes]
            zsend[side, 0, slot, span] = pick(lane, [turn(w, width * (q + 1)) for q, w in enumerate(parts)])
            zsend[side, 1, slot, span] = pick(lane, [turn(w, width * q) for q, w in enumerate(parts)])

    def unpack(pair, q, count):
        width = LANES // count
        from_left = turn(pair[0], LANES - width - width * q)
        from_right = turn(pair[1], LANES - width * q)
        return jnp.where(lane < LANES // 2, from_right, from_left)

    def to_z(part, slots, target, both=True):
        copies = []
        for side, devices, place in ((0, (right, left), own), (1, corners, other)):
            for d, device in enumerate(devices):
                sems = (zs.at[side, d, part], zr.at[side, d, part])
                copies.append(remote(zsend.at[side if both else 0, d, slots], target(d, place), *sems, device))
        return copies

    def fan(part, source, target, devices):
        return [
            remote(source, target, vs.at[part, d], vr.at[part, d], device) for d, device in enumerate(devices)
        ]

    def to_peers(part, ref):
        return fan(part, ref, ref, peers)

    def settle(copies):
        for copy in copies:
            copy.wait()

    pot_factor = scal[0]
    twice = scal[1]
    inv_count = scal[2]

    l_res.wait()
    pack(3, 0, [lambda span, q=q: wres[QUARTER * y + q, span] for q in range(QUARTER)])
    z_res = to_z(Z_RES, 3, lambda d, place: zres.at[d, y, place], False)
    h_ck.wait()
    for side, first in ((0, 2 * x), (1, 2 * (1 - x))):
        order = [(s, k, v) for s in range(2) for k in range(2) for v in range(2)]
        pack(0, side, [lambda span, s=s, k=k, v=v: hck[s, k, first + v, span] for s, k, v in order])
    z_ck = to_z(Z_CK, pl.ds(0, 1), lambda d, place: zrecv.at[d, pl.ds(0, 1), place])

    c_adj = to_x(adj.at[:, theirs], wadj.at[:, :, other], X_ADJ)
    c_bits = to_x(bits.at[theirs], wbits.at[:, other], X_BITS)
    c_pot = to_x(pot, wpot.at[other], X_POT)
    settle([h_adj, h_bits, l_pot])

    def sign_of(bit):
        return (2 * bit - 1).astype(jnp.float32) * inv_count

    def site_of(level):
        return level.astype(jnp.float32) * pot_factor * twice

    for side, first in ((0, 2 * x), (1, 2 * (1 - x))):
        order = [(k, v) for k in range(2) for v in range(2)]
        pack(1, side, [lambda span, k=k, v=v: hadj[k, first + v, span] for k, v in order])
        marks = [lambda span, v=v: sign_of(hbits[first + v, span]) for v in range(2)]
        pack(2, side, marks + [lambda span: site_of(wpot[span])] * 2)
    z_adj = to_z(Z_ADJ, pl.ds(1, 2), lambda d, place: zrecv.at[d, pl.ds(1, 2), place])

    c_res.wait()
    g_rows = to_peers(V_ROWS, wres.at[share, other])
    settle(z_res)
    g_halo = to_peers(V_HALO, zres.at[:, y])

    l_ck.wait()
    c_ck.wait()
    for j in range(DEPTH):
        planes = [wck[s, k, v, rows(j)] for s in range(2) for k in range(2) for v in range(2)]
        for q, plane in enumerate(planes):
            s, k, v = q // 4, q // 2 % 2, q % 2
            states[s * SEG + k, v, j] = plane
            (even, odd)[k][s, v, j, 0] = plane
    settle(z_ck)
    for j in range(DEPTH):
        pair = [zrecv[d, 0, rows(j)] for d in range(2)]
        for q in range(8):
            s, k, v = q // 4, q // 2 % 2, q % 2
            (even, odd)[k][s, v, j, 1] = unpack(pair, q, 8)

    settle([l_adj, l_bits, c_adj, c_bits, c_pot])
    for j in range(DEPTH):
        planes = [wadj[k, v, rows(j)] for k in range(2) for v in range(2)]
        for q, plane in enumerate(planes):
            (adj_even, adj_odd)[q // 2][q % 2, j, 0] = plane
        signs[0, j, 0] = sign_of(wbits[0, rows(j)])
        signs[1, j, 0] = sign_of(wbits[1, rows(j)])
        onsite[j, 0] = site_of(wpot[rows(j)])

    def halves(value):
        high = value.astype(jnp.bfloat16)
        return high, (value - high.astype(jnp.float32)).astype(jnp.bfloat16)

    def spread(value):
        pick_t = lax.broadcasted_iota(jnp.int32, (TERMS * 8, TERMS), 0) >> 3
        pick_t = pick_t == lax.broadcasted_iota(jnp.int32, (TERMS * 8, TERMS), 1)
        pick_e = lax.broadcasted_iota(jnp.int32, (ENERGIES, ENERGIES * 8), 1) >> 3
        pick_e = pick_e == lax.broadcasted_iota(jnp.int32, (ENERGIES, ENERGIES * 8), 0)
        same = lax.broadcasted_iota(jnp.int32, (TERMS * 8, ENERGIES * 8), 0)
        same = (same & 7) == (lax.broadcasted_iota(jnp.int32, (TERMS * 8, ENERGIES * 8), 1) & 7)
        flag = lambda mask: jnp.where(mask, 1.0, 0.0).astype(jnp.bfloat16)
        tall = jnp.dot(flag(pick_t), value, preferred_element_type=jnp.float32).astype(jnp.bfloat16)
        wide = jnp.dot(tall, flag(pick_e), preferred_element_type=jnp.float32)
        return jnp.where(same, wide, 0.0).astype(jnp.bfloat16)

    kron_high, kron_low = [spread(part) for part in halves(coefs[...])]

    kron_wide = jnp.concatenate([kron_high, kron_high], axis=1)

    def weigh(c):
        for j in range(0, DEPTH, 2):
            block = [rwin[j + i, c].reshape(ENERGIES * 8, LANES) for i in range(2)]
            high, low = halves(jnp.concatenate(block, axis=1))
            total = jnp.dot(kron_wide, jnp.concatenate([high, low], axis=0), preferred_element_type=jnp.float32)
            total = total + jnp.dot(kron_low, high, preferred_element_type=jnp.float32)
            for i in range(2):
                weights[j + i, c] = total[:, i * LANES : (i + 1) * LANES].reshape(TERMS, 8, LANES)

    settle(g_rows)
    for j in range(DEPTH):
        for e in range(ENERGIES):
            rwin[j, 0, e] = wres[e, rows(j)]
    weigh(0)

    settle(z_adj)
    for j in range(DEPTH):
        pair = [zrecv[d, 1, rows(j)] for d in range(2)]
        for q in range(4):
            (adj_even, adj_odd)[q // 2][q % 2, j, 1] = unpack(pair, q, 4)
        pair = [zrecv[d, 2, rows(j)] for d in range(2)]
        signs[0, j, 1] = unpack(pair, 0, 4)
        signs[1, j, 1] = unpack(pair, 1, 4)
        onsite[j, 1] = unpack(pair, 2, 4)

    first_lane = lane == 0
    last_lane = lane == LANES - 1

    def beside(ref, v, j):
        here = [ref[v, j, c] for c in range(2)]
        back = [pltpu.roll(w, 1, 1) for w in here]
        ahead = [pltpu.roll(w, LANES - 1, 1) for w in here]
        sums = []
        for c in range(2):
            before = jnp.where(first_lane, back[1 - c], back[c])
            after = jnp.where(last_lane, ahead[1 - c], ahead[c])
            if j == 0:
                above = pltpu.roll(ref[v, DEPTH - 1, c], 1, 0)
            else:
                above = ref[v, j - 1, c]
            if j == DEPTH - 1:
                below = pltpu.roll(ref[v, 0, c], 7, 0)
            else:
                below = ref[v, j + 1, c]
            sums.append((above + below) + (before + after))
        return here, sums

    def forward(half, carry):
        for step in range(2):
            now, then = (odd, even) if step == 0 else (even, odd)
            k = 2 + 2 * half + step
            for s in range(2):
                for v in range(2):
                    values = []
                    for j in range(DEPTH):
                        here, sums = beside(now.at[s], v, j)
                        for c in range(2):
                            values.append((onsite[j, c] * here[c] - twice * sums[c]) - then[s, v, j, c])
                    for j in range(DEPTH):
                        for c in range(2):
                            then[s, v, j, c] = values[2 * j + c]
                    for j in range(DEPTH):
                        states[s * SEG + k, v, j] = values[2 * j]
        return carry

    lax.fori_loop(0, SEG // 2 - 1, forward, 0)

    settle(g_halo)
    for j in range(DEPTH):
        for e in range(ENERGIES):
            pair = [zres[d, e // QUARTER, rows(j)] for d in range(2)]
            rwin[j, 1, e] = unpack(pair, e % QUARTER, QUARTER)
    weigh(1)

    def adjoint(part, sums_in):
        grads = list(sums_in)
        for step in range(4):
            now, then = (adj_even, adj_odd) if step % 2 == 0 else (adj_odd, adj_even)
            t = TERMS - 1 - step - 4 * part
            for v in range(2):
                values = []
                for j in range(DEPTH):
                    here, sums = beside(now, v, j)
                    grads[j] = grads[j] + here[0] * states[t, v, j]
                    for c in range(2):
                        source = weights[j, c, t] * signs[v, j, c]
                        values.append((source + onsite[j, c] * here[c]) - (twice * sums[c] + then[v, j, c]))
                for j in range(DEPTH):
                    for c in range(2):
                        then[v, j, c] = values[2 * j + c]
        return tuple(grads)

    zero = jnp.zeros((8, LANES), jnp.float32)
    grads = lax.fori_loop(0, TERMS // 4, adjoint, (zero,) * DEPTH)

    for j in range(DEPTH):
        gbuf[rows(j)] = grads[j]
        for k in range(2):
            for v in range(2):
                obuf[k, v, rows(j)] = (adj_even, adj_odd)[k][v, j, 0]
    sums = fan(V_CROSS, gbuf.at[other], gall.at[x, y], far)
    gall[x, y] = gbuf[own]
    sums += to_peers(V_GRAD, gall.at[x, y])
    c_out = to_x(obuf.at[:, :, other], adj_out.at[:, mine], X_OUT)
    l_out = local(obuf.at[:, :, own], adj_out.at[:, mine], X_OUT)
    settle(sums)
    total = gall[0, 0] + gall[1, 0]
    for d in range(1, n_y):
        total = total + (gall[0, d] + gall[1, d])
    gbuf[own] = total * twice
    l_grad = local(gbuf.at[own], grad_out, X_CK)
    l_out.wait()
    c_out.wait()
    l_grad.wait()


def windowed(
    checkpoints,
    adjoints_in,
    vector_bits,
    potential_int,
    pot_scale,
    energies,
    residual,
    first_segment,
):
    n_y = lax.axis_size("vec")
    pot_factor = pot_scale[0]
    twice = 2.0 / (4.5 + QMAX * pot_factor)
    coefficients = window_coefs(first_segment, energies)
    inv_count = 1.0 / (n_y * vector_bits.shape[0])
    scal = jnp.stack([pot_factor, twice, jnp.float32(inv_count)])
    f32, i32 = jnp.float32, jnp.int32
    vmem = pl.BlockSpec(memory_space=pltpu.VMEM)
    tile = (8, LANES)
    gradient, adjoint_out = pl.pallas_call(
        kernel,
        out_shape=(
            jax.ShapeDtypeStruct(potential_int.shape, f32),
            jax.ShapeDtypeStruct(adjoints_in.shape, f32),
        ),
        in_specs=[pl.BlockSpec(memory_space=pltpu.SMEM), vmem] + [pl.BlockSpec(memory_space=pl.ANY)] * 5,
        out_specs=(pl.BlockSpec(memory_space=pl.ANY),) * 2,
        scratch_shapes=[
            pltpu.VMEM(checkpoints.shape, f32),
            pltpu.VMEM(adjoints_in.shape, f32),
            pltpu.VMEM(vector_bits.shape, i32),
            pltpu.VMEM((2, 2, 2, 2 * ROWS, LANES), f32),
            pltpu.VMEM((2, 2, 2 * ROWS, LANES), f32),
            pltpu.VMEM((2, 2 * ROWS, LANES), i32),
            pltpu.VMEM((2 * ROWS, LANES), i32),
            pltpu.VMEM((ENERGIES, 2 * ROWS, LANES), f32),
            pltpu.VMEM((2, 2, 4, ROWS, LANES), f32),
            pltpu.VMEM((2, 3, 2 * ROWS, LANES), f32),
            pltpu.VMEM((2, n_y, 2 * ROWS, LANES), f32),
            pltpu.VMEM((TERMS, 2, DEPTH) + tile, f32),
            pltpu.VMEM((2, 2, DEPTH, 2) + tile, f32),
            pltpu.VMEM((2, 2, DEPTH, 2) + tile, f32),
            pltpu.VMEM((2, DEPTH, 2) + tile, f32),
            pltpu.VMEM((2, DEPTH, 2) + tile, f32),
            pltpu.VMEM((DEPTH, 2) + tile, f32),
            pltpu.VMEM((2, DEPTH, 2) + tile, f32),
            pltpu.VMEM((DEPTH, 2, ENERGIES) + tile, f32),
            pltpu.VMEM((DEPTH, 2, TERMS) + tile, f32),
            pltpu.VMEM((2 * ROWS, LANES), f32),
            pltpu.VMEM((2, n_y, ROWS, LANES), f32),
            pltpu.VMEM((2, 2, 2 * ROWS, LANES), f32),
            pltpu.SemaphoreType.DMA((9,)),
            pltpu.SemaphoreType.DMA((6,)),
            pltpu.SemaphoreType.DMA((6,)),
            pltpu.SemaphoreType.DMA((2, 2, 3)),
            pltpu.SemaphoreType.DMA((2, 2, 3)),
            pltpu.SemaphoreType.DMA((4, n_y)),
            pltpu.SemaphoreType.DMA((4, n_y)),
        ],
        compiler_params=pltpu.CompilerParams(
            collective_id=0, has_side_effects=True, vmem_limit_bytes=537 * 1024 * 1024 // 10
        ),
    )(scal, coefficients, checkpoints, adjoints_in, vector_bits, potential_int, residual)
    return gradient, adjoint_out


def solution(mesh):
    fits = mesh.shape["row"] == 2 and mesh.shape["col"] > 2 and mesh.shape["vec"] == 4
    return jax.shard_map(
        windowed if fits else per_device,
        mesh=mesh,
        in_specs=(
            P(None, None, "vec", "row", "col"),
            P(None, "vec", "row", "col"),
            P("vec", "row", "col"),
            P("row", "col"),
            P(),
            P(),
            P(None, "row", "col"),
            P(),
        ),
        out_specs=(P("row", "col"), P(None, "vec", "row", "col")),
        check_vma=False,
    )
```
